128 devices in a mesh: section: 2 (over y_hi), dp: 16 (over x, y_lo, core), tensor: 4 (over z).
Axes of the slice: x: 4, y: 4 (y_hi: 2, y_lo: 2; y = y_hi * 2 + y_lo), z: 4, core: 2. Of those that a mesh axis runs over, the one named last changes fastest.
Arguments:
- ends_in: bfloat16 [2, 2, 2048, 2048], P('section', None, ('dp', 'tensor')), may hold values from -6 to 6
- segments: int32 [2, 2048], P(None, 'dp'), may hold values from 0 to 4, as said below
- decay_rate: float32 [2, 8], P('section'), may hold values from 0.0001 to 0.03
- attn_gain: bfloat16 [2, 2048], P('section', 'dp'), may hold values from 0.5 to 1.5
- w_query: bfloat16 [2, 2048, 2048], P('section', 'dp', 'tensor'), may hold values from -0.125 to 0.125
- w_key: bfloat16 [2, 2048, 2048], P('section', 'dp', 'tensor'), may hold values from -0.125 to 0.125
- w_value: bfloat16 [2, 2048, 3456], P('section', 'dp', 'tensor'), may hold values from -0.125 to 0.125
- w_gate_ret: bfloat16 [2, 2048, 3456], P('section', 'dp', 'tensor'), may hold values from -0.125 to 0.125
- w_out: bfloat16 [2, 3456, 2048], P('section', 'tensor', 'dp'), may hold values from -0.109375 to 0.109375
- ffn_gain: bfloat16 [2, 2048], P('section', 'dp'), may hold values from 0.5 to 1.5
- w_gate: bfloat16 [2, 2048, 3456], P('section', 'dp', 'tensor'), may hold values from -0.125 to 0.125
- w_up: bfloat16 [2, 2048, 3456], P('section', 'dp', 'tensor'), may hold values from -0.125 to 0.125
- w_down: bfloat16 [2, 3456, 2048], P('section', 'tensor', 'dp'), may hold values from -0.109375 to 0.109375
Outputs:
- ends_out: float32 [2, 2, 2048, 2048], P('section', None, ('dp', 'tensor'))
- grad_attn_gain: float32 [2, 2048], P('section', 'dp')
- grad_query: float32 [2, 2048, 2048], P('section', 'dp', 'tensor')
- grad_key: float32 [2, 2048, 2048], P('section', 'dp', 'tensor')
- grad_value: float32 [2, 2048, 3456], P('section', 'dp', 'tensor')
- grad_gate_ret: float32 [2, 2048, 3456], P('section', 'dp', 'tensor')
- grad_out: float32 [2, 3456, 2048], P('section', 'tensor', 'dp')
- grad_ffn_gain: float32 [2, 2048], P('section', 'dp')
- grad_gate: float32 [2, 2048, 3456], P('section', 'dp', 'tensor')
- grad_up: float32 [2, 2048, 3456], P('section', 'dp', 'tensor')
- grad_down: float32 [2, 3456, 2048], P('section', 'tensor', 'dp')
The draws below stay inside these ranges and needn't reach their ends.
Inputs may be any that keep to these rules, and one draw needn't show every extreme that they name: `segments`: ids never fall along a micro-batch; in each micro-batch one document starts within its first 128 tokens and ends within its last 128 tokens.
All inputs are finite; a program needn't handle non-finite values.
Results may differ from the reference program's by a relative error of at most 0.038.
Values may be sent and summed in bfloat16 or wider, within the bound.
No kernel may reach another device: no remote copies, remote signals or barrier semaphores. Data moves between devices by JAX's collectives and lax.ppermute only.
A program may use at most 192 MiB of HBM per device.

```python
import math
import jax
import jax.numpy as jnp
from jax import lax

D = 2048
HEADS = 8
VD = 3456
FF = 3456
HEAD_K = 256
HEAD_V = 432
MICRO = 2
STRETCH = 128
TOKENS = 2048


def draw_segments(key, part):
    key = jax.random.fold_in(key, 11)
    keys_all = jax.random.split(key, 4)
    doc_start = jax.random.randint(keys_all[0], (MICRO,), 1, STRETCH)
    early_cut = jax.random.randint(keys_all[1], (MICRO,), 1, doc_start + 1)
    doc_end = jax.random.randint(keys_all[2], (MICRO,), TOKENS - STRETCH + 1, TOKENS)
    late_cut = jax.random.randint(keys_all[3], (MICRO,), doc_end, TOKENS)
    places = jnp.arange(TOKENS)[None, :]
    doc_ids = (places >= early_cut[:, None]).astype(jnp.int32)
    doc_ids = doc_ids + (places >= doc_start[:, None]).astype(jnp.int32)
    doc_ids = doc_ids + (places >= doc_end[:, None]).astype(jnp.int32)
    doc_ids = doc_ids + (places >= late_cut[:, None]).astype(jnp.int32)
    return doc_ids


def block_levels(key, dims, pieces, low, largest):
    loudness, own = 1.0, jax.random.fold_in(key, 6)
    for dim, parts in pieces:
        steps = jnp.exp(jax.random.uniform(jax.random.fold_in(own, dim), (parts,), jnp.float32, low / len(pieces), largest / len(pieces)))
        loudness = loudness * jnp.repeat(steps, dims[dim] // parts).reshape([-1 if axis == dim else 1 for axis in range(len(dims))])
    return loudness


def bell_draw(key, extent, width, reach, cuts=(), kind=jnp.bfloat16):
    gain = block_levels(key, extent, cuts, -0.22, 0.18) if cuts else 1.0
    array = jax.random.normal(key, extent, jnp.float32) * width * gain
    return jnp.minimum(jnp.maximum(array, -reach), reach).astype(kind)


def setup_inputs(seed: int = 0) -> dict:
    key_list = jax.random.split(jax.random.key(seed), 14)
    return {
        "ends_in": bell_draw(key_list[0], (2, MICRO, TOKENS, D), 1.0, 6.0, ((0, 2), (2, 64))),
        "segments": draw_segments(jax.random.fold_in(key_list[13], 71), 0),
        "decay_rate": jnp.clip(jnp.exp(math.log(0.03) - 5.7037825 * jax.random.uniform(key_list[2], (2, HEADS), jnp.float32) ** block_levels(key_list[2], (2, HEADS), ((0, 2),), -0.2, 0.2)), 0.0001, 0.03),
        "attn_gain": jnp.clip(1.0 + 0.1 * jax.random.normal(key_list[3], (2, D), jnp.float32), 0.5, 1.5).astype(jnp.bfloat16),
        "w_query": bell_draw(key_list[4], (2, D, D), D ** -0.5, 0.125, ((0, 2), (1, 16), (2, 4))),
        "w_key": bell_draw(key_list[5], (2, D, D), D ** -0.5, 0.125, ((0, 2), (1, 16), (2, 4))),
        "w_value": bell_draw(key_list[6], (2, D, VD), D ** -0.5, 0.125, ((0, 2), (1, 16), (2, 4))),
        "w_gate_ret": bell_draw(key_list[7], (2, D, VD), D ** -0.5, 0.125, ((0, 2), (1, 16), (2, 4))),
        "w_out": bell_draw(key_list[8], (2, VD, D), VD ** -0.5, 0.109375, ((0, 2), (1, 4), (2, 16))),
        "ffn_gain": jnp.clip(1.0 + 0.1 * jax.random.normal(key_list[9], (2, D), jnp.float32), 0.5, 1.5).astype(jnp.bfloat16),
        "w_gate": bell_draw(key_list[10], (2, D, FF), D ** -0.5, 0.125, ((0, 2), (1, 16), (2, 4))),
        "w_up": bell_draw(key_list[11], (2, D, FF), D ** -0.5, 0.125, ((0, 2), (1, 16), (2, 4))),
        "w_down": bell_draw(key_list[12], (2, FF, D), FF ** -0.5, 0.109375, ((0, 2), (1, 4), (2, 16))),
    }


@jax.custom_vjp
def low(v):
    return lax.optimization_barrier(v.astype(jnp.bfloat16)).astype(jnp.float32)

@jax.custom_vjp
def low_back(v):
    return v

def low_keep(v):
    return (low(v), None)

def low_pass(kept, grad):
    return (grad,)

def back_keep(v):
    return (v, None)

def back_low(kept, grad):
    return (low(grad),)
low.defvjp(low_keep, low_pass)
low_back.defvjp(back_keep, back_low)
epsilon = 1e-06
group_floor = 1.0
highest = lax.Precision.HIGHEST

def product(operand, matrix):
    return jnp.dot(operand, matrix, precision=highest)

def rms_scale(row_block, gain_vec):
    return row_block * lax.rsqrt(lax.optimization_barrier(jnp.mean(row_block * row_block, axis=-1, keepdims=True)) + epsilon) * gain_vec

def retention(queries, keys_in, values, decays, doc_ids):
    row_count = queries.shape[0]
    query_heads = queries.reshape(row_count, HEADS, HEAD_K).transpose(1, 0, 2)
    key_heads = keys_in.reshape(row_count, HEADS, HEAD_K).transpose(1, 0, 2)
    value_heads = values.reshape(row_count, HEADS, HEAD_V).transpose(1, 0, 2)
    places = jnp.arange(row_count)
    distance = places[:, None] - places[None, :]
    allowed = (distance >= 0) & (doc_ids[:, None] == doc_ids[None, :])
    span_len = jnp.where(allowed, distance, 0).astype(queries.dtype)

    def one_head(head_item):
        query_one, key_one, value_one, decay_one = head_item
        weights = jnp.where(allowed, jnp.exp(-decay_one * span_len), 0.0)
        scores = product(query_one, key_one.T) * HEAD_K ** (-0.5) * weights
        return product(scores, value_one)
    retained = lax.map(jax.checkpoint(one_head), (query_heads, key_heads, value_heads, decays))
    retained = retained * lax.rsqrt(lax.optimization_barrier(jnp.mean(retained * retained, axis=-1, keepdims=True)) + group_floor)
    return retained.transpose(1, 0, 2).reshape(row_count, HEADS * HEAD_V)

def retnet_layer(row_block, doc_ids, decays, params):
    attn_gain, w_query, w_key, w_value, w_gate_ret, w_out, ffn_gain, w_gate, w_up, w_down = params
    a_rows = low(rms_scale(row_block, attn_gain))
    queries = low_back(low(product(a_rows, w_query)))
    keys_in = low_back(low(product(a_rows, w_key)))
    values = low_back(low(product(a_rows, w_value)))
    ret_gate = low_back(product(a_rows, w_gate_ret))
    gated = low(jax.nn.silu(ret_gate) * retention(queries, keys_in, values, decays, doc_ids))
    mid_rows = row_block + low_back(product(gated, w_out))
    b_rows = low(rms_scale(mid_rows, ffn_gain))
    gate_pre = low_back(product(b_rows, w_gate))
    up_pre = low_back(product(b_rows, w_up))
    hidden = low(jax.nn.silu(gate_pre) * up_pre)
    return mid_rows + low_back(product(hidden, w_down))

def reference(ends_in, segments, decay_rate, attn_gain, w_query, w_key, w_value, w_gate_ret, w_out, ffn_gain, w_gate, w_up, w_down):
    params = tuple((weight.astype(jnp.float32) for weight in (attn_gain, w_query, w_key, w_value, w_gate_ret, w_out, ffn_gain, w_gate, w_up, w_down)))
    decays = decay_rate.astype(jnp.float32)
    totals = tuple((jnp.zeros_like(weight) for weight in params))
    grads_in = []
    outputs = []
    for micro_index in range(MICRO):
        doc_ids = segments[micro_index]

        def network(row_block, layer_params):
            first_out = retnet_layer(row_block, doc_ids, decays[0], tuple((weight[0] for weight in layer_params)))
            passed = low(low_back(first_out))
            return retnet_layer(passed, doc_ids, decays[1], tuple((weight[1] for weight in layer_params)))
        result, pullback = jax.vjp(network, ends_in[0, micro_index].astype(jnp.float32), params)
        grad_rows, grad_params = pullback(ends_in[1, micro_index].astype(jnp.float32))
        totals = tuple((running + addend for running, addend in zip(totals, grad_params)))
        grads_in.append(grad_rows)
        outputs.append(result)
    ends_out = jnp.stack([jnp.stack(grads_in), jnp.stack(outputs)])
    return (ends_out, totals[0], totals[1], totals[2], totals[3], totals[4], totals[5], totals[6], totals[7], totals[8], totals[9])
```

```python
import jax
import jax.numpy as jnp
from jax import lax
from jax.sharding import Mesh, PartitionSpec as P

epsilon = 1e-06
group_floor = 1.0
AXES = ("section", "x", "ylo", "core", "tensor")
DP = ("x", "ylo", "core")
f32 = jnp.float32
bf16 = jnp.bfloat16


def low(v):
    return v.astype(bf16)


def wide(v):
    return v.astype(f32)


def mm(a, b):
    return lax.dot_general(a, b, (((1,), (0,)), ((), ())), preferred_element_type=f32)


def mm_right(a, b):
    return lax.dot_general(a, b, (((1,), (1,)), ((), ())), preferred_element_type=f32)


def mm_left(a, b):
    return lax.dot_general(a, b, (((0,), (0,)), ((), ())), preferred_element_type=f32)


def swap(v, axis):
    return lax.ppermute(v, axis, [(0, 1), (1, 0)])


def cross(v):
    return lax.ppermute(v, ("section", "ylo"), [(0, 3), (1, 2), (2, 1), (3, 0)])


def turn(v, axis, by):
    n = lax.axis_size(axis)
    return lax.ppermute(v, axis, [(i, (i + by) % n) for i in range(n)])


def shift(v, axis, by):
    n = lax.axis_size(axis)
    return lax.ppermute(v, axis, [(i, i + by) for i in range(n) if 0 <= i + by < n])


def spread(rows):
    n = lax.axis_size("tensor")
    parts = [rows] + [turn(rows, "tensor", -k) for k in range(1, n)]
    own = jnp.concatenate(parts)
    return jnp.concatenate([own, swap(own, "core")])


def collect(partial):
    n = lax.axis_size("tensor")
    half = partial.shape[0] // 2
    share = half // n
    own = partial[:half] + wide(swap(low(partial[half:]), "core"))
    total = own[:share]
    for k in range(1, n):
        total = total + wide(turn(low(own[k * share : (k + 1) * share]), "tensor", k))
    return total


def pick(flag, a, b):
    return jnp.where(flag, a, b)


def side(flag, a, b):
    return jnp.where(flag == 0, jnp.concatenate([a, b]), jnp.concatenate([b, a]))


def rms_inverse(x):
    return lax.rsqrt(jnp.mean(x * x, axis=-1, keepdims=True) + epsilon)


def norm_back(x, gain, d_y):
    r = rms_inverse(x)
    gd = gain * d_y
    d_x = r * gd - x * (r * r * r) * jnp.mean(x * gd, axis=-1, keepdims=True)
    return d_x, jnp.sum(x * r * d_y, axis=0)


def earlier_states(state, ctx):
    fade = ctx["fade"]
    sent = low(state)
    other = wide(swap(sent, "ylo"))
    own = wide(sent)
    y = ctx["ylo"]
    first, second = pick(y == 0, own, other), pick(y == 0, other, own)
    pair = low(fade * first + second)
    total = wide(shift(pair, "x", 1))
    total = total + (fade**2) * wide(shift(pair, "x", 2)) + (fade**4) * wide(shift(pair, "x", 3))
    return pick(y == 0, total, fade * total + first)


def later_states(state, ctx):
    fade = ctx["fade"]
    sent = low(state)
    other = wide(swap(sent, "ylo"))
    own = wide(sent)
    y = ctx["ylo"]
    first, second = pick(y == 0, own, other), pick(y == 0, other, own)
    pair = low(first + fade * second)
    total = wide(shift(pair, "x", -1))
    total = total + (fade**2) * wide(shift(pair, "x", -2)) + (fade**4) * wide(shift(pair, "x", -3))
    return pick(y == 1, total, second + fade * total)


def silu(v):
    return v * jax.nn.sigmoid(v)


def forward(h, a_rows, ffn_gain, weights, ctx):
    w_kv, w_qg, w_out, w_gu, w_down = weights
    K, V, F = ctx["sizes"]
    kv = mm(a_rows, w_kv)
    k, v = low(kv[:, :K]), low(kv[:, K : K + V])
    faded_k = low(wide(k) * ctx["to_end"])
    state_in = low(earlier_states(mm_left(faded_k, v), ctx))
    qg = mm(a_rows, w_qg)
    q, ret_gate = low(qg[:, :K]), qg[:, K:]
    scores = low(mm_right(q, k) * ctx["decay_mask"])
    retained = mm(scores, v) + mm(q, state_in) * ctx["from_start"]
    n = lax.rsqrt(jnp.mean(retained * retained, axis=-1, keepdims=True) + group_floor)
    gated = low(silu(ret_gate) * (retained * n))
    mid = h + collect(mm_right(gated, w_out))
    b_rows = spread(low(mid * rms_inverse(mid) * ffn_gain))
    gu = mm(b_rows, w_gu)
    gate_pre, up_pre = gu[:, :F], gu[:, F:]
    hidden = low(silu(gate_pre) * up_pre)
    out = mid + collect(mm_right(hidden, w_down))
    record = (a_rows, k, v, q, state_in, scores, ret_gate, retained, gated, mid, b_rows, gu, hidden)
    return out, record


def backward(h, g_out, d_f, record, gains, weights, ctx):
    w_kv, w_qg, w_out, w_gu, w_down = weights
    attn_gain, ffn_gain = gains
    K, V, F = ctx["sizes"]
    a_rows, k, v, q, state_in, scores, ret_gate, retained, gated, mid, b_rows, gu, hidden = record
    d_hidden = mm(d_f, w_down)
    gate_pre, up_pre = gu[:, :F], gu[:, F:]
    s = jax.nn.sigmoid(gate_pre)
    d_gate = low(d_hidden * up_pre * s * (1.0 + gate_pre * (1.0 - s)))
    d_up = low(d_hidden * gate_pre * s)
    d_gu = jnp.concatenate([d_gate, d_up], axis=1)
    d_b = collect(mm_right(d_gu, w_gu))
    grad_down = low(mm_left(d_f, hidden))
    grad_gu = low(mm_left(b_rows, d_gu))
    d_norm, grad_ffn_gain = norm_back(mid, ffn_gain, d_b)
    d_mid = g_out + d_norm
    d_r = spread(low(d_mid))
    d_gated = mm(d_r, w_out)
    s = jax.nn.sigmoid(ret_gate)
    n = lax.rsqrt(jnp.mean(retained * retained, axis=-1, keepdims=True) + group_floor)
    d_ret_gate = low(d_gated * (retained * n) * s * (1.0 + ret_gate * (1.0 - s)))
    d_normed = d_gated * ret_gate * s
    d_ret = n * d_normed - retained * (n * n * n) * jnp.mean(
        retained * d_normed, axis=-1, keepdims=True
    )
    d_ret_low = low(d_ret)
    d_ret_start = low(d_ret * ctx["from_start"])
    beyond = low(later_states(mm_left(q, d_ret_start), ctx))
    grad_out = low(mm_left(d_r, gated))
    d_scores = low(mm_right(d_ret_low, v) * ctx["decay_mask"])
    d_q = low(mm(d_scores, k) + mm_right(d_ret_start, state_in))
    d_qg = jnp.concatenate([d_q, d_ret_gate], axis=1)
    grad_qg = low(mm_left(a_rows, d_qg))
    d_k = low(mm_left(d_scores, q) + mm_right(v, beyond) * ctx["to_end"])
    d_v = low(mm_left(scores, d_ret_low) + mm(k, beyond) * ctx["to_end"])
    d_kv = jnp.concatenate([d_k, d_v], axis=1)
    grad_kv = low(mm_left(a_rows, d_kv))
    d_kv_wide = jnp.pad(d_kv, ((0, 0), (0, w_kv.shape[1] - d_kv.shape[1])))
    d_a = collect(mm_right(d_qg, w_qg) + mm_right(d_kv_wide, w_kv))
    d_norm, grad_attn_gain = norm_back(h, attn_gain, d_a)
    return d_mid + d_norm, (grad_kv, grad_qg, grad_out, grad_gu, grad_down), (grad_attn_gain, grad_ffn_gain)


def halves(w, core):
    n = w.shape[1] // 2
    first, second = w[:, :n], w[:, n:]
    return pick(core == 0, first, second), pick(core == 0, second, first)


def bring(shards, ctx):
    core, section, ylo = ctx["core"], ctx["section"], ctx["ylo"]
    split = [halves(w, core) for w in shards]
    keep = jnp.concatenate([a for a, _ in split], axis=1)
    give = jnp.concatenate([b for _, b in split], axis=1)
    own = side(core, keep, swap(give, "core"))
    own_other = swap(own, "ylo")
    far_other = cross(own)
    far = swap(far_other, "ylo")
    mine = side(ylo, own, own_other)
    theirs = side(ylo, far, far_other)
    return pick(section == 0, mine, theirs), pick(section == 0, theirs, mine)


def gather_x(rows):
    return lax.all_gather(rows, "x", axis=0, tiled=True)


def settle(grad, layer, ctx):
    part = lax.psum_scatter(grad, "x", scatter_dimension=0, tiled=True)
    half = part.shape[0] // 2
    away = ctx["section"] != layer
    place = jnp.where(away, 1 - ctx["ylo"], ctx["ylo"])
    keep = pick(place == 0, part[:half], part[half:])
    give = pick(place == 0, part[half:], part[:half])
    total = wide(keep) + wide(swap(give, "ylo"))
    return total + wide(cross(low(total)))


def share_out(total, ctx):
    core = ctx["core"]
    half = total.shape[0] // 2
    keep = pick(core == 0, total[:half], total[half:])
    give = pick(core == 0, total[half:], total[:half])
    return keep, wide(swap(low(give), "core"))


def both(pair, lo, hi, ctx):
    keep, other = pair
    a, b = keep[:, lo:hi], other[:, lo:hi]
    return jnp.where(ctx["core"] == 0, jnp.concatenate([a, b], 1), jnp.concatenate([b, a], 1))


def body(
    ends_in,
    segments,
    decay_rate,
    attn_gain,
    w_query,
    w_key,
    w_value,
    w_gate_ret,
    w_out,
    ffn_gain,
    w_gate,
    w_up,
    w_down,
):
    section, core, tensor = (lax.axis_index(a) for a in ("section", "core", "tensor"))
    x_at, ylo = lax.axis_index("x"), lax.axis_index("ylo")
    K, V, F = w_query.shape[2] // 2, w_value.shape[2] // 2, w_gate.shape[2] // 2
    D = w_query.shape[1] * lax.axis_size("x") * 4

    ends = ends_in[0]
    mine = pick(section == 0, ends[0], ends[1])
    theirs = swap(pick(section == 0, ends[1], ends[0]), "section")
    h0 = pick(section == 0, mine, theirs)
    g1 = pick(section == 0, theirs, mine)

    stretch = segments.shape[1]
    rows = 2 * stretch
    share = stretch // lax.axis_size("tensor")
    own_docs = pick(section == 0, segments[0], segments[1])
    ring = (tensor * share + jnp.arange(stretch)) % stretch
    own_docs = lax.dynamic_slice_in_dim(jnp.concatenate([own_docs, own_docs]), tensor * share, stretch)
    docs = jnp.concatenate([own_docs, swap(own_docs, "core")])
    places = jnp.concatenate([core * stretch + ring, (1 - core) * stretch + ring])
    block = x_at * 2 + ylo
    scale = K ** (-0.5)

    decays_all = decay_rate[0]
    decays_far = swap(decays_all, "section")
    head = tensor * 2 + core

    def context(layer):
        rates = pick(section == layer, decays_all, decays_far)
        rate = lax.dynamic_index_in_dim(rates, head, 0, False)
        gap = places[:, None] - places[None, :]
        allowed = (gap >= 0) & (docs[:, None] == docs[None, :])
        decay_mask = jnp.where(allowed, jnp.exp(-rate * jnp.where(allowed, gap, 0).astype(f32)), 0.0) * scale
        to_end = jnp.exp(-rate * (rows - 1 - places).astype(f32)) * (docs == jnp.max(docs))
        linked = (docs == jnp.min(docs)) & (block > 0)
        from_start = jnp.exp(-rate * (places + 1).astype(f32)) * linked * scale
        return {
            "decay_mask": decay_mask,
            "to_end": to_end[:, None],
            "from_start": from_start[:, None],
            "fade": jnp.exp(-rate * rows),
            "ylo": ylo,
            "core": core,
            "section": section,
            "sizes": (K, V, F),
        }

    ctxs = (context(0), context(1))
    ctx = ctxs[0]

    gain_columns = jnp.stack([attn_gain[0], ffn_gain[0]], axis=1)
    gain_columns = jnp.concatenate([gain_columns, gain_columns], axis=1)
    kv0, kv1 = bring((w_key[0], w_value[0], gain_columns), ctx)
    qg0, qg1 = bring((w_query[0], w_gate_ret[0]), ctx)
    out0, out1 = bring((w_out[0].T,), ctx)
    gu0, gu1 = bring((w_gate[0], w_up[0]), ctx)
    down0, down1 = bring((w_down[0].T,), ctx)
    weights0 = tuple(gather_x(w) for w in (kv0, qg0, out0, gu0, down0))
    weights1 = tuple(gather_x(w) for w in (kv1, qg1, out1, gu1, down1))

    def gains_of(weights):
        columns = wide(weights[0][:, K + V : K + V + 2]).T
        return columns[0], columns[1]

    gains0, gains1 = gains_of(weights0), gains_of(weights1)

    h0_rows = wide(spread(h0))
    a0 = low(h0_rows * rms_inverse(h0_rows) * gains0[0])
    h0 = wide(h0)
    out_first, record0 = forward(h0, a0, gains0[1], weights0, ctxs[0])
    h1 = wide(low(out_first))
    a1 = spread(low(h1 * rms_inverse(h1) * gains1[0]))
    out_second, record1 = forward(h1, a1, gains1[1], weights1, ctxs[1])

    d_f1 = spread(g1)
    d_h1, grads1, gain_grads1 = backward(
        h1, wide(g1), d_f1, record1, gains1, weights1, ctxs[1]
    )
    settled1 = [settle(g, 1, ctx) for g in grads1]
    d_f0_rows = low(d_h1)
    d_h0, grads0, gain_grads0 = backward(
        h0, wide(d_f0_rows), spread(d_f0_rows), record0, gains0, weights0, ctxs[0]
    )
    settled0 = [settle(g, 0, ctx) for g in grads0]

    shared = [share_out(pick(section == 0, a, b), ctx) for a, b in zip(settled0, settled1)]
    kv, qg, out, gu, down = shared
    grad_key = both(kv, 0, K, ctx)
    grad_value = both(kv, K, K + V, ctx)
    grad_query = both(qg, 0, K, ctx)
    grad_gate_ret = both(qg, K, K + V, ctx)
    grad_out = both(out, 0, V, ctx).T
    grad_gate = both(gu, 0, F, ctx)
    grad_up = both(gu, F, 2 * F, ctx)
    grad_down = both(down, 0, F, ctx).T

    gain_grads = jnp.stack(gain_grads0 + gain_grads1)
    for axis, order in (
        ("tensor", ((0, 1), (1, 0), (2, 3), (3, 2))),
        ("tensor", ((0, 3), (3, 0), (1, 2), (2, 1))),
        ("core", ((0, 1), (1, 0))),
        ("x", ((0, 1), (1, 0), (2, 3), (3, 2))),
        ("x", ((0, 3), (3, 0), (1, 2), (2, 1))),
        ("ylo", ((0, 1), (1, 0))),
        ("section", ((0, 1), (1, 0))),
    ):
        gain_grads = gain_grads + lax.ppermute(gain_grads, axis, order)
    own_gains = pick(section == 0, gain_grads[:2], gain_grads[2:])
    width = attn_gain.shape[1]
    own_gains = lax.dynamic_slice_in_dim(own_gains, (block * 2 + core) * width, width, 1)

    kept = pick(section == 0, d_h0, out_second)
    passed = swap(pick(section == 0, out_second, d_h0), "section")
    ends_out = jnp.where(section == 0, jnp.stack([kept, passed]), jnp.stack([passed, kept]))
    return (
        ends_out[None],
        own_gains[:1],
        grad_query[None],
        grad_key[None],
        grad_value[None],
        grad_gate_ret[None],
        grad_out[None],
        own_gains[1:],
        grad_gate[None],
        grad_up[None],
        grad_down[None],
    )


def solution(mesh):
    fine = Mesh(mesh.devices.reshape(2, 4, 2, 2, 4), AXES)
    by_rows = P("section", DP, "tensor")
    by_columns = P("section", "tensor", DP)
    ends = P("section", None, DP + ("tensor",), None)
    gain = P("section", DP)
    return jax.shard_map(
        body,
        mesh=fine,
        in_specs=(
            ends,
            P(None, DP),
            P("section", None),
            gain,
            by_rows,
            by_rows,
            by_rows,
            by_rows,
            by_columns,
            gain,
            by_rows,
            by_rows,
            by_columns,
        ),
        out_specs=(
            ends,
            gain,
            by_rows,
            by_rows,
            by_rows,
            by_rows,
            by_columns,
            gain,
            by_rows,
            by_rows,
            by_columns,
        ),
        check_vma=False,
    )
```

```python
import jax
import jax.numpy as jnp
from jax import lax
from jax.experimental.layout import Layout, with_layout_constraint
from jax.sharding import Mesh, PartitionSpec as P

epsilon = 1e-06
group_floor = 1.0
AXES = ("section", "x", "ylo", "core", "tensor")
DP = ("x", "ylo", "core")
f32 = jnp.float32
bf16 = jnp.bfloat16


def low(v):
    return v.astype(bf16)


def wide(v):
    return v.astype(f32)


def row_major(v):
    return with_layout_constraint(v, Layout(major_to_minor=tuple(range(v.ndim))))


def mm(a, b):
    return lax.dot_general(a, b, (((1,), (0,)), ((), ())), preferred_element_type=f32)


def mm_right(a, b):
    return lax.dot_general(a, b, (((1,), (1,)), ((), ())), preferred_element_type=f32)


def mm_left(a, b):
    return lax.dot_general(a, b, (((0,), (0,)), ((), ())), preferred_element_type=f32)


def swap(v, axis):
    return lax.ppermute(v, axis, [(0, 1), (1, 0)])


def cross(v):
    return lax.ppermute(v, ("section", "ylo"), [(0, 3), (1, 2), (2, 1), (3, 0)])


def turn(v, axis, by):
    n = lax.axis_size(axis)
    return lax.ppermute(v, axis, [(i, (i + by) % n) for i in range(n)])


def shift(v, axis, by):
    n = lax.axis_size(axis)
    return lax.ppermute(v, axis, [(i, i + by) for i in range(n) if 0 <= i + by < n])


def spread(rows):
    with jax.named_scope("spread"):
        return spread_rows(rows)


def collect(partial):
    with jax.named_scope("collect"):
        return collect_rows(partial)


def spread_rows(rows):
    n = lax.axis_size("tensor")
    rows = row_major(rows)
    parts = [rows] + [row_major(turn(rows, "tensor", -k)) for k in range(1, n)]
    own = row_major(jnp.concatenate(parts))
    return row_major(jnp.concatenate([own, row_major(swap(own, "core"))]))


def collect_rows(partial):
    n = lax.axis_size("tensor")
    half = partial.shape[0] // 2
    share = half // n
    partial = row_major(partial)
    own = row_major(partial[:half] + wide(swap(row_major(low(partial[half:])), "core")))
    total = own[:share]
    for k in range(1, n):
        total = total + wide(turn(row_major(low(own[k * share : (k + 1) * share])), "tensor", k))
    return row_major(total)


def pick(flag, a, b):
    return jnp.where(flag, a, b)


def side(flag, a, b):
    return jnp.where(flag == 0, jnp.concatenate([a, b]), jnp.concatenate([b, a]))


def rms_inverse(x):
    return lax.rsqrt(jnp.mean(x * x, axis=-1, keepdims=True) + epsilon)


def norm_back(x, gain, d_y):
    r = rms_inverse(x)
    gd = gain * d_y
    d_x = r * gd - x * (r * r * r) * jnp.mean(x * gd, axis=-1, keepdims=True)
    return d_x, jnp.sum(x * r * d_y, axis=0)


def earlier_states(state, ctx):
    with jax.named_scope("earlier_states"):
        return states_before(state, ctx)


def later_states(state, ctx):
    with jax.named_scope("later_states"):
        return states_after(state, ctx)


def states_before(state, ctx):
    fade = ctx["fade"]
    sent = low(state)
    got = swap(sent, "ylo")
    other = wide(got)
    own = wide(sent)
    y = ctx["ylo"]
    first, second = pick(y == 0, own, other), pick(y == 0, other, own)
    pair = low(fade * first + second)
    total = wide(shift(pair, "x", 1))
    total = total + (fade**2) * wide(shift(pair, "x", 2)) + (fade**4) * wide(shift(pair, "x", 3))
    return pick(y == 0, total, fade * total + first), got


def states_after(state, ctx):
    fade = ctx["fade"]
    sent = low(state)
    other = wide(swap(sent, "ylo"))
    own = wide(sent)
    y = ctx["ylo"]
    first, second = pick(y == 0, own, other), pick(y == 0, other, own)
    pair = low(first + fade * second)
    total = wide(shift(pair, "x", -1))
    total = total + (fade**2) * wide(shift(pair, "x", -2)) + (fade**4) * wide(shift(pair, "x", -3))
    return pick(y == 1, total, second + fade * total)


def silu(v):
    return v * jax.nn.sigmoid(v)


def forward(h, a_rows, ffn_gain, weights, ctx, waits=()):
    w_kv, w_qgo, get_gud = weights
    K, V, F = ctx["sizes"]
    kv = mm(a_rows, w_kv)
    k, v = low(kv[:, :K]), low(kv[:, K : K + V])
    faded_k = low(wide(k) * ctx["to_end"])
    state_in, swapped = earlier_states(mm_left(faded_k, v), ctx)
    state_in = low(state_in)
    w_gud = get_gud(swapped)
    w_gu, w_down = w_gud[:, : 2 * F], w_gud[:, 2 * F :]
    w_qg, w_out = w_qgo[:, : K + V], w_qgo[:, K + V :]
    qg = mm(a_rows, w_qg)
    q, ret_gate = low(qg[:, :K]), qg[:, K:]
    scores = low(mm_right(q, k) * ctx["decay_mask"])
    retained = mm(scores, v) + mm(q, state_in) * ctx["from_start"]
    n = lax.rsqrt(jnp.mean(retained * retained, axis=-1, keepdims=True) + group_floor)
    gated = low(silu(ret_gate) * (retained * n))
    mid = h + collect(mm_right(gated, w_out))
    b_rows = spread(low(mid * rms_inverse(mid) * ffn_gain))
    pairs, _ = swap_halves((a_rows, b_rows), (), ctx)
    gu = mm(b_rows, w_gu)
    gate_pre, up_pre = gu[:, :F], gu[:, F:]
    hidden = hold(low(silu(gate_pre) * up_pre), *waits)
    _, rights = swap_halves((), (gated, hidden), ctx)
    out = mid + collect(mm_right(hidden, w_down))
    record = (pairs, rights, k, v, q, state_in, scores, ret_gate, retained, mid, gu)
    return out, record, (w_kv, w_qg, w_out, w_gu, w_down)


def backward(h, g_out, d_f_rows, record, gains, weights, ctx, merged, waits=((), (), ())):
    w_kv, w_qg, w_out, w_gu, w_down = weights
    attn_gain, ffn_gain = gains
    K, V, F = ctx["sizes"]
    (a_pair, b_pair), (gated_pair, hidden_pair), k, v, q, state_in, scores, ret_gate, retained, mid, gu = record
    d_f = spread(d_f_rows)
    (f_pair,), _ = swap_halves((d_f,), (), ctx)
    d_hidden = mm(d_f, w_down)
    gate_pre, up_pre = gu[:, :F], gu[:, F:]
    s = jax.nn.sigmoid(gate_pre)
    d_gate = low(d_hidden * up_pre * s * (1.0 + gate_pre * (1.0 - s)))
    d_up = low(d_hidden * gate_pre * s)
    d_gu = jnp.concatenate([d_gate, d_up], axis=1)
    d_b = collect(mm_right(d_gu, w_gu))
    _, (gu_pair,) = swap_halves((), (d_gu,), ctx)
    part_down = settle(weight_grad(f_pair, hidden_pair))
    part_gu = settle(weight_grad(b_pair, gu_pair))
    d_b = hold(d_b, *waits[0])
    d_norm, grad_ffn_gain = norm_back(mid, ffn_gain, d_b)
    d_mid = g_out + d_norm
    d_r = spread(low(d_mid))
    (r_pair,), _ = swap_halves((d_r,), (), ctx)
    d_gated = mm(d_r, w_out)
    s = jax.nn.sigmoid(ret_gate)
    n = lax.rsqrt(jnp.mean(retained * retained, axis=-1, keepdims=True) + group_floor)
    d_ret_gate = low(d_gated * (retained * n) * s * (1.0 + ret_gate * (1.0 - s)))
    d_normed = d_gated * ret_gate * s
    d_ret = n * d_normed - retained * (n * n * n) * jnp.mean(
        retained * d_normed, axis=-1, keepdims=True
    )
    d_ret_low = low(d_ret)
    d_ret_start = low(d_ret * ctx["from_start"])
    beyond = low(later_states(mm_left(q, d_ret_start), ctx))
    part_out = settle(weight_grad(r_pair, gated_pair))
    d_scores = low(mm_right(d_ret_low, v) * ctx["decay_mask"])
    d_q = low(mm(d_scores, k) + mm_right(d_ret_start, state_in))
    d_qg = jnp.concatenate([d_q, d_ret_gate], axis=1)
    _, (qg_pair,) = swap_halves((), (d_qg,), ctx)
    beyond = hold(beyond, *waits[1])
    if not merged:
        part_qg = settle(weight_grad(a_pair, qg_pair))
    d_k = low(mm_left(d_scores, q) + mm_right(v, beyond) * ctx["to_end"])
    d_v = low(mm_left(scores, d_ret_low) + mm(k, beyond) * ctx["to_end"])
    d_kv = jnp.concatenate([d_k, d_v], axis=1)
    d_kv_wide = jnp.pad(d_kv, ((0, 0), (0, w_kv.shape[1] - d_kv.shape[1])))
    partial = mm_right(d_qg, w_qg) + mm_right(d_kv_wide, w_kv)
    d_a = collect(partial)
    _, (kv_pair,) = swap_halves((), (d_kv,), ctx)
    if merged:
        pair = tuple(jnp.concatenate(p, axis=1) for p in zip(kv_pair, qg_pair))
        part_in = settle(weight_grad(a_pair, pair))
        part_kv, part_qg = part_in[:, : K + V], part_in[:, K + V :]
    else:
        part_kv = settle(weight_grad(a_pair, kv_pair))
        d_a = hold(d_a, part_down, part_gu)
    d_norm, grad_attn_gain = norm_back(h, attn_gain, d_a)
    parts = (part_kv, part_qg, part_out, part_gu, part_down)
    return d_mid + d_norm, parts, (grad_attn_gain, grad_ffn_gain)


def swap_halves(lefts, rights, ctx):
    n = lax.axis_size("x")

    def half(v, which):
        width = v.shape[1] // (2 * n)
        cut = [v[:, i * width : (i + 1) * width] for i in range(2 * n)]
        return jnp.concatenate([pick(which == 0, cut[2 * i], cut[2 * i + 1]) for i in range(n)], axis=1)

    place = ctx["place"]
    keeps = [half(v, place) for v in lefts]
    sent = jnp.concatenate([half(v, 1 - place) for v in lefts] + list(rights), axis=1)
    got = swap(sent, "ylo")
    at, left_pairs, right_pairs = 0, [], []
    for keep in keeps:
        left_pairs.append((keep, got[:, at : at + keep.shape[1]]))
        at += keep.shape[1]
    for right in rights:
        right_pairs.append((right, got[:, at : at + right.shape[1]]))
        at += right.shape[1]
    return left_pairs, right_pairs


def weight_grad(left, right):
    return row_major(low(mm_left(left[0], right[0]) + mm_left(left[1], right[1])))


def halves(w, core):
    n = w.shape[1] // 2
    first, second = w[:, :n], w[:, n:]
    return pick(core == 0, first, second), pick(core == 0, second, first)


def corner(v):
    return v[tuple(slice(n - 1, n) for n in v.shape)].reshape(1, 1)


def hold(v, *others):
    if not others:
        return v
    corners = [corner(other) for other in others]
    bad = corners[0] != corners[0]
    for c in corners[1:]:
        bad = bad | (c != c)
    return jnp.where(bad, jnp.zeros((), v.dtype), v)


def gather_x(rows):
    return lax.all_gather(rows, "x", axis=0, tiled=True)


def pack(shards, ctx):
    split = [halves(w, ctx["core"]) for w in shards]
    keep = jnp.concatenate([a for a, _ in split], axis=1)
    give = jnp.concatenate([b for _, b in split], axis=1)
    return side(ctx["core"], keep, swap(give, "core"))


def along_y(own):
    return swap(own, "ylo"), cross(own), swap(own, "section")


def both_layers(own, moved, ctx):
    near, crossed, facing = moved
    section, at_0 = ctx["section"], ctx["ylo"] == 0
    mine = (pick(at_0, own, near), pick(at_0, near, own))
    theirs = (pick(at_0, facing, crossed), pick(at_0, crossed, facing))
    first = [pick(section == 0, a, b) for a, b in zip(mine, theirs)]
    second = [pick(section == 0, b, a) for a, b in zip(mine, theirs)]
    return first, second


def y_then_x(own, moved, ctx, ready=()):
    first, second = both_layers(own, moved, ctx)
    return hold(jnp.concatenate(first), *ready), jnp.concatenate(second)


def settle(grad):
    return lax.psum_scatter(grad, "x", scatter_dimension=0, tiled=True)


def share_out(first, second, ctx):
    section, core = ctx["section"], ctx["core"]
    total = wide(pick(section == 0, first, second)) + wide(cross(pick(section == 0, second, first)))
    half = total.shape[0] // 2
    keep = pick(core == 0, total[:half], total[half:])
    give = pick(core == 0, total[half:], total[:half])
    return keep, wide(swap(low(give), "core"))


def both(pair, lo, hi, ctx):
    keep, other = pair
    a, b = keep[:, lo:hi], other[:, lo:hi]
    return jnp.where(ctx["core"] == 0, jnp.concatenate([a, b], 1), jnp.concatenate([b, a], 1))


def body(
    ends_in,
    segments,
    decay_rate,
    attn_gain,
    w_query,
    w_key,
    w_value,
    w_gate_ret,
    w_out,
    ffn_gain,
    w_gate,
    w_up,
    w_down,
):
    section, core, tensor = (lax.axis_index(a) for a in ("section", "core", "tensor"))
    x_at, ylo = lax.axis_index("x"), lax.axis_index("ylo")
    K, V, F = w_query.shape[2] // 2, w_value.shape[2] // 2, w_gate.shape[2] // 2
    D = w_query.shape[1] * lax.axis_size("x") * 4

    ends = ends_in[0]
    mine = pick(section == 0, ends[0], ends[1])
    theirs = swap(pick(section == 0, ends[1], ends[0]), "section")
    h0 = pick(section == 0, mine, theirs)
    g1 = pick(section == 0, theirs, mine)

    stretch = segments.shape[1]
    rows = 2 * stretch
    share = stretch // lax.axis_size("tensor")
    own_docs = pick(section == 0, segments[0], segments[1])
    ring = (tensor * share + jnp.arange(stretch)) % stretch
    own_docs = lax.dynamic_slice_in_dim(jnp.concatenate([own_docs, own_docs]), tensor * share, stretch)
    docs = jnp.concatenate([own_docs, swap(own_docs, "core")])
    places = jnp.concatenate([core * stretch + ring, (1 - core) * stretch + ring])
    block = x_at * 2 + ylo
    scale = K ** (-0.5)

    decays_all = decay_rate[0]
    decays_far = swap(decays_all, "section")
    head = tensor * 2 + core

    def context(layer):
        rates = pick(section == layer, decays_all, decays_far)
        rate = lax.dynamic_index_in_dim(rates, head, 0, False)
        gap = places[:, None] - places[None, :]
        allowed = (gap >= 0) & (docs[:, None] == docs[None, :])
        decay_mask = jnp.where(allowed, jnp.exp(-rate * jnp.where(allowed, gap, 0).astype(f32)), 0.0) * scale
        to_end = jnp.exp(-rate * (rows - 1 - places).astype(f32)) * (docs == jnp.max(docs))
        linked = (docs == jnp.min(docs)) & (block > 0)
        from_start = jnp.exp(-rate * (places + 1).astype(f32)) * linked * scale
        return {
            "decay_mask": decay_mask,
            "to_end": to_end[:, None],
            "from_start": from_start[:, None],
            "fade": jnp.exp(-rate * rows),
            "place": jnp.where(section == layer, ylo, 1 - ylo),
            "ylo": ylo,
            "core": core,
            "section": section,
            "sizes": (K, V, F),
        }

    ctxs = (context(0), context(1))
    ctx = ctxs[0]

    gain_columns = jnp.stack([attn_gain[0], ffn_gain[0]], axis=1)
    gain_columns = jnp.concatenate([gain_columns, gain_columns], axis=1)
    h0_rows = wide(spread(h0))
    with jax.named_scope("weights_key_value"):
        own_kv = pack((w_key[0], w_value[0], gain_columns), ctx)
        ready = (h0_rows, ctxs[0]["decay_mask"], ctxs[1]["decay_mask"])
        kv0, kv1 = y_then_x(own_kv, along_y(own_kv), ctx, ready)
    with jax.named_scope("weights_query_gate_out"):
        own_qgo = hold(pack((w_query[0], w_gate_ret[0], w_out[0].T), ctx), kv0)
        qgo0, qgo1 = y_then_x(own_qgo, along_y(own_qgo), ctx)
    with jax.named_scope("gather_weights"):
        kv0, kv1 = gather_x(kv0), gather_x(kv1)
        qgo0, qgo1 = gather_x(qgo0), gather_x(qgo1)
    second = []

    def get_gud(swapped):
        with jax.named_scope("weights_gate_up_down"):
            own_gud = hold(pack((w_gate[0], w_up[0], w_down[0].T), ctx), swapped)
            gud0, gud1 = y_then_x(own_gud, along_y(own_gud), ctx)
            second.append(gather_x(gud1))
            return gather_x(gud0)

    def gain_rows(columns):
        columns = wide(columns).T
        return columns[0], columns[1]

    gains0 = gain_rows(kv0[:, K + V : K + V + 2])
    gains1 = gain_rows(kv1[:, K + V : K + V + 2])
    weights0 = (kv0, qgo0, get_gud)
    weights1 = (kv1, qgo1, lambda swapped: second[0])

    a0 = low(h0_rows * rms_inverse(h0_rows) * gains0[0])
    h0 = wide(h0)
    with jax.named_scope("layer0_forward"):
        out_first, record0, weights0 = forward(h0, a0, gains0[1], weights0, ctxs[0])
    h1 = wide(low(out_first))
    a1 = spread(low(h1 * rms_inverse(h1) * gains1[0]))
    early = [pair[1] for pair in record0[0] + record0[1]]
    with jax.named_scope("layer1_forward"):
        out_second, record1, weights1 = forward(h1, a1, gains1[1], weights1, ctxs[1], early)

    with jax.named_scope("layer1_backward"):
        d_h1, parts1, gain_grads1 = backward(
            h1, wide(g1), g1, record1, gains1, weights1, ctxs[1], True
        )
    d_f0 = low(d_h1)
    kv1, qg1, out1, gu1, down1 = parts1
    with jax.named_scope("layer0_backward"):
        d_h0, parts0, gain_grads0 = backward(
            h0, wide(d_f0), d_f0, record0, gains0, weights0, ctxs[0], False, ((gu1, down1), (out1, kv1))
        )
    kv0, qg0, out0, gu0, down0 = parts0
    with jax.named_scope("owners"):
        kv, qg, out, gu, down = (
            share_out(a, b, ctx)
            for a, b in ((kv0, kv1), (qg0, qg1), (out0, out1), (gu0, gu1), (down0, down1))
        )
    grad_key = both(kv, 0, K, ctx)
    grad_value = both(kv, K, K + V, ctx)
    grad_query = both(qg, 0, K, ctx)
    grad_gate_ret = both(qg, K, K + V, ctx)
    grad_out = both(out, 0, V, ctx).T
    grad_gate = both(gu, 0, F, ctx)
    grad_up = both(gu, F, 2 * F, ctx)
    grad_down = both(down, 0, F, ctx).T

    gain_grads = jnp.stack(gain_grads0 + gain_grads1)
    with jax.named_scope("gains"):
        for moves in (
            [lambda v, k=k: turn(v, "tensor", k) for k in (1, 2, 3)],
            [lambda v: swap(v, "core")],
            [lambda v, k=k: turn(v, "x", k) for k in (1, 2, 3)],
            [lambda v: swap(v, "ylo"), cross, lambda v: swap(v, "section")],
        ):
            gain_grads = gain_grads + sum(move(gain_grads) for move in moves)
    own_gains = pick(section == 0, gain_grads[:2], gain_grads[2:])
    width = attn_gain.shape[1]
    own_gains = lax.dynamic_slice_in_dim(own_gains, (block * 2 + core) * width, width, 1)

    kept = pick(section == 0, d_h0, out_second)
    passed = swap(pick(section == 0, out_second, d_h0), "section")
    ends_out = jnp.where(section == 0, jnp.stack([kept, passed]), jnp.stack([passed, kept]))
    return (
        ends_out[None],
        own_gains[:1],
        grad_query[None],
        grad_key[None],
        grad_value[None],
        grad_gate_ret[None],
        grad_out[None],
        own_gains[1:],
        grad_gate[None],
        grad_up[None],
        grad_down[None],
    )


def solution(mesh):
    fine = Mesh(mesh.devices.reshape(2, 4, 2, 2, 4), AXES)
    by_rows = P("section", DP, "tensor")
    by_columns = P("section", "tensor", DP)
    ends = P("section", None, DP + ("tensor",), None)
    gain = P("section", DP)
    return jax.shard_map(
        body,
        mesh=fine,
        in_specs=(
            ends,
            P(None, DP),
            P("section", None),
            gain,
            by_rows,
            by_rows,
            by_rows,
            by_rows,
            by_columns,
            gain,
            by_rows,
            by_rows,
            by_columns,
        ),
        out_specs=(
            ends,
            gain,
            by_rows,
            by_rows,
            by_rows,
            by_rows,
            by_columns,
            gain,
            by_rows,
            by_rows,
            by_columns,
        ),
        check_vma=False,
    )
```

```python
import jax
import jax.numpy as jnp
from jax import lax
from jax.experimental.layout import Layout, with_layout_constraint
from jax.sharding import Mesh, PartitionSpec as P

epsilon = 1e-06
group_floor = 1.0
AXES = ("section", "x", "ylo", "core", "tensor")
DP = ("x", "ylo", "core")
f32 = jnp.float32
bf16 = jnp.bfloat16


def low(v):
    return v.astype(bf16)


def wide(v):
    return v.astype(f32)


def row_major(v):
    return with_layout_constraint(v, Layout(major_to_minor=tuple(range(v.ndim))))


def columns_major(v):
    return with_layout_constraint(v, Layout(major_to_minor=(1, 0)))


def mm(a, b):
    return lax.dot_general(a, b, (((1,), (0,)), ((), ())), preferred_element_type=f32)


def mm_right(a, b):
    return lax.dot_general(a, b, (((1,), (1,)), ((), ())), preferred_element_type=f32)


def mm_left(a, b):
    return lax.dot_general(a, b, (((0,), (0,)), ((), ())), preferred_element_type=f32)


def swap(v, axis):
    return lax.ppermute(v, axis, [(0, 1), (1, 0)])


def cross(v):
    return lax.ppermute(v, ("section", "ylo"), [(0, 3), (1, 2), (2, 1), (3, 0)])


def turn(v, axis, by):
    n = lax.axis_size(axis)
    return lax.ppermute(v, axis, [(i, (i + by) % n) for i in range(n)])


def shift(v, axis, by):
    n = lax.axis_size(axis)
    return lax.ppermute(v, axis, [(i, i + by) for i in range(n) if 0 <= i + by < n])


def spread(rows):
    with jax.named_scope("spread"):
        return spread_rows(rows)


def collect(partial):
    with jax.named_scope("collect"):
        return collect_rows(partial)


def spread_rows(rows):
    n = lax.axis_size("tensor")
    rows = row_major(rows)
    parts = [rows] + [row_major(turn(rows, "tensor", -k)) for k in range(1, n)]
    own = row_major(jnp.concatenate(parts))
    return row_major(jnp.concatenate([own, row_major(swap(own, "core"))]))


def collect_rows(partial):
    n = lax.axis_size("tensor")
    half = partial.shape[0] // 2
    share = half // n
    partial = row_major(partial)
    own = row_major(partial[:half] + wide(swap(row_major(low(partial[half:])), "core")))
    total = own[:share]
    for k in range(1, n):
        total = total + wide(turn(row_major(low(own[k * share : (k + 1) * share])), "tensor", k))
    return row_major(total)


def pick(flag, a, b):
    return jnp.where(flag, a, b)


def side(flag, a, b):
    return jnp.where(flag == 0, jnp.concatenate([a, b]), jnp.concatenate([b, a]))


def rms_inverse(x):
    return lax.rsqrt(jnp.mean(x * x, axis=-1, keepdims=True) + epsilon)


def norm_back(x, gain, d_y):
    r = rms_inverse(x)
    gd = gain * d_y
    d_x = r * gd - x * (r * r * r) * jnp.mean(x * gd, axis=-1, keepdims=True)
    return d_x, jnp.sum(x * r * d_y, axis=0)


def earlier_states(state, ctx):
    with jax.named_scope("earlier_states"):
        return states_before(state, ctx)


def later_states(state, ctx):
    with jax.named_scope("later_states"):
        return states_after(state, ctx)


def states_before(state, ctx):
    fade = ctx["fade"]
    sent = low(state)
    got = swap(sent, "ylo")
    other = wide(got)
    own = wide(sent)
    y = ctx["ylo"]
    first, second = pick(y == 0, own, other), pick(y == 0, other, own)
    pair = low(fade * first + second)
    total = wide(shift(pair, "x", 1))
    total = total + (fade**2) * wide(shift(pair, "x", 2)) + (fade**4) * wide(shift(pair, "x", 3))
    return pick(y == 0, total, fade * total + first), pair


def states_after(state, ctx):
    fade = ctx["fade"]
    sent = low(state)
    other = wide(swap(sent, "ylo"))
    own = wide(sent)
    y = ctx["ylo"]
    first, second = pick(y == 0, own, other), pick(y == 0, other, own)
    pair = low(first + fade * second)
    total = wide(shift(pair, "x", -1))
    total = total + (fade**2) * wide(shift(pair, "x", -2)) + (fade**4) * wide(shift(pair, "x", -3))
    return pick(y == 1, total, second + fade * total)


def silu(v):
    return v * jax.nn.sigmoid(v)


def forward(h, a_rows, ffn_gain, weights, ctx, waits=()):
    w_in, w_out, get_gud = weights
    K, V, F = ctx["sizes"]
    split = len(w_in) == 2
    kv = mm(a_rows, w_in[0])
    k, v = low(kv[:, :K]), low(kv[:, K : K + V])
    faded_k = low(wide(k) * ctx["to_end"])
    state_in, pair = earlier_states(mm_left(faded_k, v), ctx)
    state_in = low(state_in)
    w_gud = get_gud(pair)
    w_gu, w_down = w_gud[:, : 2 * F], w_gud[:, 2 * F :]
    qg = mm(a_rows, w_in[1]) if split else kv[:, K + V :]
    q, ret_gate = low(qg[:, :K]), qg[:, K:]
    scores = low(mm_right(q, k) * ctx["decay_mask"])
    retained = mm(scores, v) + mm(q, state_in) * ctx["from_start"]
    n = lax.rsqrt(jnp.mean(retained * retained, axis=-1, keepdims=True) + group_floor)
    gated = low(silu(ret_gate) * (retained * n))
    mid = h + collect(mm_right(gated, w_out))
    b_rows = spread(low(mid * rms_inverse(mid) * ffn_gain))
    gu = mm(b_rows, w_gu)
    gate_pre, up_pre = gu[:, :F], gu[:, F:]
    hidden = hold(low(silu(gate_pre) * up_pre), *waits)
    record = (a_rows, b_rows, gated, hidden, k, v, q, state_in, scores, ret_gate, retained, mid, gu)
    return record, (w_in, w_out, w_gu, w_down)


def layer_out(record, weights):
    hidden, mid = record[3], record[-2]
    return mid + collect(mm_right(hidden, weights[-1]))


def backward(h, g_out, d_f_rows, record, pairs, gains, weights, ctx, waits):
    a_pair, b_pair = pairs
    w_in, w_out, w_gu, w_down = weights
    attn_gain, ffn_gain = gains
    K, V, F = ctx["sizes"]
    a_rows, b_rows, gated, hidden, k, v, q, state_in, scores, ret_gate, retained, mid, gu = record
    d_f = spread(d_f_rows)
    d_hidden = mm(d_f, w_down)
    gate_pre, up_pre = gu[:, :F], gu[:, F:]
    s = jax.nn.sigmoid(gate_pre)
    d_gate = low(d_hidden * up_pre * s * (1.0 + gate_pre * (1.0 - s)))
    d_up = low(d_hidden * gate_pre * s)
    d_gu = jnp.concatenate([d_gate, d_up], axis=1)
    d_b = collect(mm_right(d_gu, w_gu))
    part_gu = settle(weight_grad(b_pair, d_gu))
    d_b = hold(d_b, *waits[0])
    d_norm, grad_ffn_gain = norm_back(mid, ffn_gain, d_b)
    d_mid = g_out + d_norm
    d_r = spread(low(d_mid))
    d_gated = mm(d_r, w_out)
    s = jax.nn.sigmoid(ret_gate)
    n = lax.rsqrt(jnp.mean(retained * retained, axis=-1, keepdims=True) + group_floor)
    d_ret_gate = low(d_gated * (retained * n) * s * (1.0 + ret_gate * (1.0 - s)))
    d_normed = d_gated * ret_gate * s
    d_ret = n * d_normed - retained * (n * n * n) * jnp.mean(
        retained * d_normed, axis=-1, keepdims=True
    )
    d_ret_low = low(d_ret)
    d_ret_start = low(d_ret * ctx["from_start"])
    beyond = low(later_states(mm_left(q, d_ret_start), ctx))
    grad_od = [row_major(low(mm_left(left, right))) for left, right in ((d_r, gated), (d_f, hidden))]
    part_od = settle(jnp.concatenate(grad_od, axis=1))
    beyond = hold(beyond, *waits[1](part_gu))
    d_scores = low(mm_right(d_ret_low, v) * ctx["decay_mask"])
    d_q = low(mm(d_scores, k) + mm_right(d_ret_start, state_in))
    d_qg = jnp.concatenate([d_q, d_ret_gate], axis=1)
    if len(w_in) == 2:
        part_qg = settle(weight_grad(a_pair, d_qg))
    d_k = low(mm_left(d_scores, q) + mm_right(v, beyond) * ctx["to_end"])
    d_v = low(mm_left(scores, d_ret_low) + mm(k, beyond) * ctx["to_end"])
    d_kv = jnp.concatenate([d_k, d_v], axis=1)
    if len(w_in) == 2:
        d_kv_wide = jnp.pad(d_kv, ((0, 0), (0, w_in[0].shape[1] - d_kv.shape[1])))
        d_a = collect(mm_right(d_qg, w_in[1]) + mm_right(d_kv_wide, w_in[0]))
        grad_kv = weight_grad(a_pair, d_kv)
        part_kv = settle(grad_kv)
        d_a = hold(d_a, grad_kv, *waits[2](part_qg))
    else:
        d_in = jnp.concatenate([d_kv, d_qg], axis=1)
        d_a = collect(mm_right(d_in, w_in[0]))
        part_in = settle(weight_grad(a_pair, d_in))
        part_kv, part_qg = part_in[:, : K + V], part_in[:, K + V :]
    d_norm, grad_attn_gain = norm_back(h, attn_gain, d_a)
    parts = (part_kv, part_qg, part_od, part_gu)
    return d_mid + d_norm, parts, (grad_attn_gain, grad_ffn_gain)


def halves(w, core):
    n = w.shape[1] // 2
    first, second = w[:, :n], w[:, n:]
    return pick(core == 0, first, second), pick(core == 0, second, first)


def swap_half(v, ctx):
    n = lax.axis_size("x")
    width = v.shape[1] // (2 * n)
    cut = [v[:, i * width : (i + 1) * width] for i in range(2 * n)]

    def half(which):
        return jnp.concatenate([pick(which == 0, cut[2 * i], cut[2 * i + 1]) for i in range(n)], axis=1)

    place = ctx["place"]
    return half(place), swap(half(1 - place), "ylo")


def weight_grad(left, right):
    return row_major(low(mm_left(left[0], right) + mm_left(left[1], swap(right, "ylo"))))


def corner(v):
    return v[tuple(slice(n - 1, n) for n in v.shape)].reshape(1, 1)


def hold(v, *others):
    if not others:
        return v
    corners = [corner(other) for other in others]
    bad = corners[0] != corners[0]
    for c in corners[1:]:
        bad = bad | (c != c)
    return jnp.where(bad, jnp.zeros((), v.dtype), v)


def gather_x(rows):
    return lax.all_gather(rows, "x", axis=0, tiled=True)


def pack(shards, ctx):
    split = [halves(w, ctx["core"]) for w in shards]
    keep = jnp.concatenate([a for a, _ in split], axis=1)
    give = jnp.concatenate([b for _, b in split], axis=1)
    return side(ctx["core"], keep, swap(give, "core"))


def along_y(own):
    return swap(own, "ylo"), cross(own), swap(own, "section")


def both_layers(own, moved, ctx):
    near, crossed, facing = moved
    section, at_0 = ctx["section"], ctx["ylo"] == 0
    mine = (pick(at_0, own, near), pick(at_0, near, own))
    theirs = (pick(at_0, facing, crossed), pick(at_0, crossed, facing))
    first = [pick(section == 0, a, b) for a, b in zip(mine, theirs)]
    second = [pick(section == 0, b, a) for a, b in zip(mine, theirs)]
    return first, second


def y_then_x(own, moved, ctx, ready=()):
    first, second = both_layers(own, moved, ctx)
    return hold(jnp.concatenate(first), *ready), jnp.concatenate(second)


def settle(grad):
    return lax.psum_scatter(row_major(grad), "x", scatter_dimension=0, tiled=True)


def sum_along_y(first, second, ctx):
    section, at_0 = ctx["section"], ctx["ylo"] == 0
    half = first.shape[0] // 2
    mine, theirs = pick(section == 0, first, second), pick(section == 0, second, first)
    keep, near = pick(at_0, mine[:half], mine[half:]), pick(at_0, mine[half:], mine[:half])
    facing, crossed = pick(at_0, theirs[:half], theirs[half:]), pick(at_0, theirs[half:], theirs[:half])
    return wide(keep) + wide(swap(near, "ylo")) + wide(swap(facing, "section")) + wide(cross(crossed))


def sum_across(first, second, ctx):
    section = ctx["section"]
    return wide(pick(section == 0, first, second)) + wide(cross(pick(section == 0, second, first)))


def share_out(total, ctx):
    core = ctx["core"]
    half = total.shape[0] // 2
    keep = pick(core == 0, total[:half], total[half:])
    give = pick(core == 0, total[half:], total[:half])
    return keep, wide(swap(low(give), "core"))


def both(pair, lo, hi, ctx):
    keep, other = pair
    a, b = keep[:, lo:hi], other[:, lo:hi]
    return jnp.where(ctx["core"] == 0, jnp.concatenate([a, b], 1), jnp.concatenate([b, a], 1))


def body(
    ends_in,
    segments,
    decay_rate,
    attn_gain,
    w_query,
    w_key,
    w_value,
    w_gate_ret,
    w_out,
    ffn_gain,
    w_gate,
    w_up,
    w_down,
):
    section, core, tensor = (lax.axis_index(a) for a in ("section", "core", "tensor"))
    x_at, ylo = lax.axis_index("x"), lax.axis_index("ylo")
    K, V, F = w_query.shape[2] // 2, w_value.shape[2] // 2, w_gate.shape[2] // 2
    D = w_query.shape[1] * lax.axis_size("x") * 4

    ends = ends_in[0]
    mine = pick(section == 0, ends[0], ends[1])
    theirs = swap(pick(section == 0, ends[1], ends[0]), "section")
    h0 = pick(section == 0, mine, theirs)
    g1 = pick(section == 0, theirs, mine)

    stretch = segments.shape[1]
    rows = 2 * stretch
    share = stretch // lax.axis_size("tensor")
    own_docs = pick(section == 0, segments[0], segments[1])
    ring = (tensor * share + jnp.arange(stretch)) % stretch
    own_docs = lax.dynamic_slice_in_dim(jnp.concatenate([own_docs, own_docs]), tensor * share, stretch)
    docs = jnp.concatenate([own_docs, swap(own_docs, "core")])
    places = jnp.concatenate([core * stretch + ring, (1 - core) * stretch + ring])
    block = x_at * 2 + ylo
    scale = K ** (-0.5)

    decays_all = decay_rate[0]
    decays_far = swap(decays_all, "section")
    head = tensor * 2 + core

    def context(layer, docs, rates_ready=()):
        rates = hold(pick(section == layer, decays_all, decays_far)[None], *rates_ready)[0]
        rate = lax.dynamic_index_in_dim(rates, head, 0, False)
        gap = places[:, None] - places[None, :]
        allowed = (gap >= 0) & (docs[:, None] == docs[None, :])
        decay_mask = jnp.where(allowed, jnp.exp(-rate * jnp.where(allowed, gap, 0).astype(f32)), 0.0) * scale
        to_end = jnp.exp(-rate * (rows - 1 - places).astype(f32)) * (docs == jnp.max(docs))
        linked = (docs == jnp.min(docs)) & (block > 0)
        from_start = jnp.exp(-rate * (places + 1).astype(f32)) * linked * scale
        return {
            "decay_mask": decay_mask,
            "to_end": to_end[:, None],
            "from_start": from_start[:, None],
            "fade": jnp.exp(-rate * rows),
            "place": jnp.where(section == layer, ylo, 1 - ylo),
            "ylo": ylo,
            "core": core,
            "section": section,
            "sizes": (K, V, F),
        }

    ctx = {"ylo": ylo, "core": core, "section": section}

    gain_columns = jnp.stack([attn_gain[0], ffn_gain[0]], axis=1)
    gain_columns = jnp.concatenate([gain_columns, gain_columns], axis=1)
    with jax.named_scope("weights_key_value"):
        own_kv = pack((w_key[0], w_value[0], gain_columns), ctx)
        kv0, kv1 = y_then_x(own_kv, along_y(own_kv), ctx)
        kv0 = jnp.concatenate([kv0, kv1[:, K + V :]], axis=1)
    with jax.named_scope("weights_query_gate_out"):
        own_qgo = hold(pack((w_query[0], w_gate_ret[0], w_out[0].T), ctx), kv0)
        moved_qgo = along_y(own_qgo)
    h0_rows = wide(spread(hold(h0, moved_qgo[0])))
    ctx0 = context(0, docs)
    with jax.named_scope("weights_query_gate_out"):
        qgo0, qgo1 = y_then_x(own_qgo, moved_qgo, ctx, (h0_rows, ctx0["decay_mask"]))
    with jax.named_scope("gather_weights"):
        kv0, qgo0 = gather_x(kv0), gather_x(qgo0)
        in1 = gather_x(jnp.concatenate([kv1[:, : K + V], qgo1], axis=1))
    second = []

    def get_gud(pair):
        with jax.named_scope("weights_gate_up_down"):
            own_gud = columns_major(pack((w_gate[0], w_up[0], w_down[0].T), ctx))
            moved_gud = [columns_major(v) for v in along_y(own_gud)]
            gud0, gud1 = y_then_x(own_gud, moved_gud, ctx, (pair,))
            second.append(gather_x(gud1))
            return gather_x(gud0)

    gain_rows = wide(kv0[:, K + V :]).T
    gains0, gains1 = gain_rows[:2], gain_rows[2:]
    n_in = 2 * (K + V)
    weights0 = ((kv0, qgo0[:, : K + V]), qgo0[:, K + V :], get_gud)
    weights1 = ((in1[:, :n_in],), in1[:, n_in:], lambda pair: second[0])

    a0 = low(h0_rows * rms_inverse(h0_rows) * gains0[0])
    h0 = wide(h0)
    with jax.named_scope("layer0_forward"):
        record0, weights0 = forward(h0, a0, gains0[1], weights0, ctx0)
        out_first = layer_out(record0, weights0)
    h1 = wide(low(out_first))
    a1 = spread(low(h1 * rms_inverse(h1) * gains1[0]))
    ctx1 = context(1, docs, (h1,))
    pairs0 = swap_half(a0, ctx0), swap_half(record0[1], ctx0)
    early = [pair[1] for pair in pairs0]
    with jax.named_scope("layer1_forward"):
        record1, weights1 = forward(h1, a1, gains1[1], weights1, ctx1, early)
    pairs1 = swap_half(a1, ctx1), swap_half(record1[1], ctx1)

    with jax.named_scope("layer1_out"):
        out_second = layer_out(record1, weights1)
    with jax.named_scope("layer1_backward"):
        waits = (pairs1[0][1:], lambda part: (out_second, part))
        d_h1, parts1, gain_grads1 = backward(
            h1, wide(g1), hold(g1, h1), record1, pairs1, gains1, weights1, ctx1, waits
        )
    d_f0 = low(d_h1)
    kv1, qg1, od1, gu1 = parts1
    sums = {}

    def sum_gu(part):
        sums["gu"] = sum_across(part, gu1, ctx)
        return (sums["gu"],)

    def sum_qg(part):
        sums["qg"] = sum_across(part, qg1, ctx)
        return (sums["qg"],)

    with jax.named_scope("layer0_backward"):
        waits = ((od1, kv1), sum_gu, sum_qg)
        d_h0, parts0, gain_grads0 = backward(
            h0, wide(d_f0), d_f0, record0, pairs0, gains0, weights0, ctx0, waits
        )
    kv0, qg0, od0, gu0 = parts0
    gain_grads = jnp.stack(gain_grads0 + gain_grads1)

    def reduce_gains(*moves):
        with jax.named_scope("gains"):
            return gain_grads + sum(move(gain_grads) for move in moves)

    with jax.named_scope("owners"):
        gain_grads = reduce_gains(*(lambda v, k=k: turn(v, "tensor", k) for k in (1, 2, 3)))
        gain_grads = reduce_gains(lambda v: swap(v, "core"))
        gain_grads = reduce_gains(*(lambda v, k=k: turn(v, "x", k) for k in (1, 2, 3)))
        kv = sum_across(kv0, kv1, ctx)
        gain_grads = hold(reduce_gains(lambda v: swap(v, "ylo"), cross, lambda v: swap(v, "section")), kv)
        od = sum_along_y(od0, od1, ctx)
        kv, qg, od, gu = (share_out(total, ctx) for total in (kv, sums["qg"], od, sums["gu"]))
    grad_key = both(kv, 0, K, ctx)
    grad_value = both(kv, K, K + V, ctx)
    grad_query = both(qg, 0, K, ctx)
    grad_gate_ret = both(qg, K, K + V, ctx)
    grad_out = both(od, 0, V, ctx).T
    grad_down = both(od, V, V + F, ctx).T
    grad_gate = both(gu, 0, F, ctx)
    grad_up = both(gu, F, 2 * F, ctx)

    own_gains = pick(section == 0, gain_grads[:2], gain_grads[2:])
    width = attn_gain.shape[1]
    own_gains = lax.dynamic_slice_in_dim(own_gains, (block * 2 + core) * width, width, 1)

    kept = pick(section == 0, d_h0, out_second)
    passed = swap(pick(section == 0, out_second, d_h0), "section")
    ends_out = jnp.where(section == 0, jnp.stack([kept, passed]), jnp.stack([passed, kept]))
    return (
        ends_out[None],
        own_gains[:1],
        grad_query[None],
        grad_key[None],
        grad_value[None],
        grad_gate_ret[None],
        grad_out[None],
        own_gains[1:],
        grad_gate[None],
        grad_up[None],
        grad_down[None],
    )


def solution(mesh):
    fine = Mesh(mesh.devices.reshape(2, 4, 2, 2, 4), AXES)
    by_rows = P("section", DP, "tensor")
    by_columns = P("section", "tensor", DP)
    ends = P("section", None, DP + ("tensor",), None)
    gain = P("section", DP)
    return jax.shard_map(
        body,
        mesh=fine,
        in_specs=(
            ends,
            P(None, DP),
            P("section", None),
            gain,
            by_rows,
            by_rows,
            by_rows,
            by_rows,
            by_columns,
            gain,
            by_rows,
            by_rows,
            by_columns,
        ),
        out_specs=(
            ends,
            gain,
            by_rows,
            by_rows,
            by_rows,
            by_rows,
            by_columns,
            gain,
            by_rows,
            by_rows,
            by_columns,
        ),
        check_vma=False,
    )
```

```python
import jax
import jax.numpy as jnp
from jax import lax
from jax.experimental import pallas as pl
from jax.experimental.layout import Layout, with_layout_constraint
from jax.sharding import Mesh, PartitionSpec as P

epsilon = 1e-06
group_floor = 1.0
AXES = ("section", "x", "ylo", "core", "tensor")
DP = ("x", "ylo", "core")
f32 = jnp.float32
bf16 = jnp.bfloat16


def low(v):
    return v.astype(bf16)


def wide(v):
    return v.astype(f32)


def row_major(v):
    return with_layout_constraint(v, Layout(major_to_minor=tuple(range(v.ndim))))


def columns_major(v):
    return with_layout_constraint(v, Layout(major_to_minor=(1, 0)))


def mm(a, b):
    return lax.dot_general(a, b, (((1,), (0,)), ((), ())), preferred_element_type=f32)


def mm_right(a, b):
    return lax.dot_general(a, b, (((1,), (1,)), ((), ())), preferred_element_type=f32)


def mm_left(a, b):
    return lax.dot_general(a, b, (((0,), (0,)), ((), ())), preferred_element_type=f32)


def swap(v, axis):
    return lax.ppermute(v, axis, [(0, 1), (1, 0)])


def cross(v):
    return lax.ppermute(v, ("section", "ylo"), [(0, 3), (1, 2), (2, 1), (3, 0)])


def turn(v, axis, by):
    n = lax.axis_size(axis)
    return lax.ppermute(v, axis, [(i, (i + by) % n) for i in range(n)])


def shift(v, axis, by):
    n = lax.axis_size(axis)
    return lax.ppermute(v, axis, [(i, i + by) for i in range(n) if 0 <= i + by < n])


def spread(rows):
    with jax.named_scope("spread"):
        return spread_rows(rows)


def collect(partial):
    with jax.named_scope("collect"):
        return collect_rows(partial)


def spread_rows(rows):
    n = lax.axis_size("tensor")
    rows = row_major(rows)
    parts = [rows] + [row_major(turn(rows, "tensor", -k)) for k in range(1, n)]
    own = row_major(jnp.concatenate(parts))
    return row_major(jnp.concatenate([own, row_major(swap(own, "core"))]))


def collect_rows(partial):
    n = lax.axis_size("tensor")
    half = partial.shape[0] // 2
    share = half // n
    partial = row_major(partial)
    own = row_major(partial[:half] + wide(swap(row_major(low(partial[half:])), "core")))
    total = own[:share]
    for k in range(1, n):
        total = total + wide(turn(row_major(low(own[k * share : (k + 1) * share])), "tensor", k))
    return row_major(total)


def pick(flag, a, b):
    return jnp.where(flag, a, b)


def side(flag, a, b):
    return jnp.where(flag == 0, jnp.concatenate([a, b]), jnp.concatenate([b, a]))


def rms_inverse(x):
    return lax.rsqrt(jnp.mean(x * x, axis=-1, keepdims=True) + epsilon)


def norm_back(x, gain, d_y):
    r = rms_inverse(x)
    gd = gain * d_y
    d_x = r * gd - x * (r * r * r) * jnp.mean(x * gd, axis=-1, keepdims=True)
    return d_x, jnp.sum(x * r * d_y, axis=0)


def earlier_states(state, ctx):
    with jax.named_scope("earlier_states"):
        return states_before(state, ctx)


def later_states(state, ctx):
    with jax.named_scope("later_states"):
        return states_after(state, ctx)


def states_before(state, ctx):
    fade = ctx["fade"]
    sent = low(state)
    got = swap(sent, "ylo")
    other = wide(got)
    own = wide(sent)
    y = ctx["ylo"]
    first, second = pick(y == 0, own, other), pick(y == 0, other, own)
    pair = low(fade * first + second)
    total = wide(shift(pair, "x", 1))
    total = total + (fade**2) * wide(shift(pair, "x", 2)) + (fade**4) * wide(shift(pair, "x", 3))
    return pick(y == 0, total, fade * total + first), pair


def states_after(state, ctx):
    fade = ctx["fade"]
    sent = low(state)
    other = wide(swap(sent, "ylo"))
    own = wide(sent)
    y = ctx["ylo"]
    first, second = pick(y == 0, own, other), pick(y == 0, other, own)
    pair = low(first + fade * second)
    total = wide(shift(pair, "x", -1))
    total = total + (fade**2) * wide(shift(pair, "x", -2)) + (fade**4) * wide(shift(pair, "x", -3))
    return pick(y == 1, total, second + fade * total)


def silu(v):
    return v * jax.nn.sigmoid(v)


def forward(h, a_rows, ffn_gain, weights, ctx, waits=((), ())):
    w_in, w_out, get_gud = weights
    K, V, F = ctx["sizes"]
    split = len(w_in) == 2
    kv = mm(a_rows, w_in[0])
    k, v = low(kv[:, :K]), low(kv[:, K : K + V])
    faded_k = low(wide(k) * ctx["to_end"])
    state_in, pair = earlier_states(mm_left(faded_k, v), ctx)
    state_in = low(state_in)
    w_gud = get_gud(pair)
    w_gu, w_down = w_gud[:, : 2 * F], w_gud[:, 2 * F :]
    qg = mm(a_rows, w_in[1]) if split else kv[:, K + V :]
    q, ret_gate = low(qg[:, :K]), qg[:, K:]
    scores = low(mm_right(q, k) * ctx["decay_mask"])
    retained = mm(scores, v) + mm(q, state_in) * ctx["from_start"]
    n = lax.rsqrt(jnp.mean(retained * retained, axis=-1, keepdims=True) + group_floor)
    gated = low(silu(ret_gate) * (retained * n))
    mid = hold(h + collect(mm_right(gated, w_out)), *waits[0])
    b_rows = hold(spread(low(mid * rms_inverse(mid) * ffn_gain)), *waits[1])
    gu = mm(b_rows, w_gu)
    gate_pre, up_pre = gu[:, :F], gu[:, F:]
    hidden = low(silu(gate_pre) * up_pre)
    record = (a_rows, b_rows, gated, hidden, k, v, q, state_in, scores, ret_gate, retained, mid, gu)
    return record, (w_in, w_out, w_gu, w_down)


def layer_out(record, weights):
    hidden, mid = record[3], record[-2]
    return mid + collect(mm_right(hidden, weights[-1]))


def backward(h, g_out, d_f, record, pairs, gains, weights, ctx, waits):
    a_pair, b_pair, f_pair, gated_pair, hidden_pair = pairs
    w_in, w_out, w_gu, w_down = weights
    attn_gain, ffn_gain = gains
    K, V, F = ctx["sizes"]
    a_rows, b_rows, gated, hidden, k, v, q, state_in, scores, ret_gate, retained, mid, gu = record
    split = len(w_in) == 2
    parts = {}
    d_hidden = mm(d_f, w_down)
    gate_pre, up_pre = gu[:, :F], gu[:, F:]
    s = jax.nn.sigmoid(gate_pre)
    d_gate = low(d_hidden * up_pre * s * (1.0 + gate_pre * (1.0 - s)))
    d_up = low(d_hidden * gate_pre * s)
    d_gu = jnp.concatenate([d_gate, d_up], axis=1)
    gu_pair = with_partner(d_gu)
    d_b = hold(collect(mm_right(d_gu, w_gu)), gu_pair[1], *waits[0](parts))
    parts["gu"] = settle(weight_grad(b_pair, gu_pair))
    d_norm, grad_ffn_gain = norm_back(mid, ffn_gain, d_b)
    d_mid = g_out + d_norm
    d_r = hold(spread(low(d_mid)), *waits[1](parts))
    r_pair = swap_half(d_r, ctx)
    d_gated = mm(d_r, w_out)
    s = jax.nn.sigmoid(ret_gate)
    n = lax.rsqrt(jnp.mean(retained * retained, axis=-1, keepdims=True) + group_floor)
    d_ret_gate = low(d_gated * (retained * n) * s * (1.0 + ret_gate * (1.0 - s)))
    d_normed = d_gated * ret_gate * s
    d_ret = n * d_normed - retained * (n * n * n) * jnp.mean(
        retained * d_normed, axis=-1, keepdims=True
    )
    d_ret_low = low(d_ret)
    d_ret_start = low(d_ret * ctx["from_start"])
    beyond = low(later_states(mm_left(q, d_ret_start), ctx))
    d_scores = low(mm_right(d_ret_low, v) * ctx["decay_mask"])
    d_q = low(mm(d_scores, k) + mm_right(d_ret_start, state_in))
    d_qg = jnp.concatenate([d_q, d_ret_gate], axis=1)
    grads = [weight_grad(r_pair, gated_pair), weight_grad(f_pair, hidden_pair)]
    swapped = [r_pair[1]]
    if split:
        qg_pair = with_partner(d_qg)
        swapped.append(qg_pair[1])
        grads.append(weight_grad(a_pair, qg_pair))
    grad_od = row_major(jnp.concatenate(grads, axis=1))
    parts["od"] = settle(grad_od)
    beyond = hold(beyond, *swapped, *waits[2](parts))
    d_k = low(mm_left(d_scores, q) + mm_right(v, beyond) * ctx["to_end"])
    d_v = low(mm_left(scores, d_ret_low) + mm(k, beyond) * ctx["to_end"])
    d_kv = jnp.concatenate([d_k, d_v], axis=1)
    d_in = d_kv if split else jnp.concatenate([d_kv, d_qg], axis=1)
    if split:
        d_kv_wide = jnp.pad(d_kv, ((0, 0), (0, w_in[0].shape[1] - d_kv.shape[1])))
        partial = mm_right(d_qg, w_in[1]) + mm_right(d_kv_wide, w_in[0])
    else:
        partial = mm_right(d_in, w_in[0])
    in_pair = with_partner(d_in)
    parts["in_partner"] = in_pair[1]
    if split:
        in_pair = in_pair[0], hold(in_pair[1], grad_od)
    parts["grad_in"] = weight_grad(a_pair, in_pair)
    parts["in"] = settle(parts["grad_in"])
    d_a = hold(collect(partial), *waits[3](parts))
    d_norm, grad_attn_gain = norm_back(h, attn_gain, d_a)
    return d_mid + d_norm, parts, (grad_attn_gain, grad_ffn_gain)


def with_partner(v):
    return v, swap(v, "ylo")


def swap_half(v, ctx):
    n = lax.axis_size("x")
    width = v.shape[1] // (2 * n)
    cut = [v[:, i * width : (i + 1) * width] for i in range(2 * n)]

    def half(which):
        return jnp.concatenate([pick(which == 0, cut[2 * i], cut[2 * i + 1]) for i in range(n)], axis=1)

    place = ctx["place"]
    return half(place), swap(half(1 - place), "ylo")


def weight_grad(left, right):
    return row_major(low(mm_left(left[0], right[0]) + mm_left(left[1], right[1])))


def halves(w, core):
    n = w.shape[1] // 2
    first, second = w[:, :n], w[:, n:]
    return pick(core == 0, first, second), pick(core == 0, second, first)


def hold(v, *others):
    if not others:
        return v
    anywhere = pl.BlockSpec(memory_space=pl.ANY)
    return pl.pallas_call(
        lambda *refs: None,
        out_shape=jax.ShapeDtypeStruct(v.shape, v.dtype),
        in_specs=[anywhere] * (1 + len(others)),
        out_specs=anywhere,
        input_output_aliases={0: 0},
        cost_estimate=pl.CostEstimate(flops=0, bytes_accessed=0, transcendentals=0),
    )(v, *others)


def corner(v):
    return v[tuple(slice(n - 1, n) for n in v.shape)].reshape(1, 1)


def hold_by_corner(v, *others):
    if not others:
        return v
    corners = [corner(other) for other in others]
    bad = corners[0] != corners[0]
    for c in corners[1:]:
        bad = bad | (c != c)
    return jnp.where(bad, jnp.zeros((), v.dtype), v)


def gather_x(rows):
    return lax.all_gather(rows, "x", axis=0, tiled=True)


def pack(shards, ctx):
    split = [halves(w, ctx["core"]) for w in shards]
    keep = jnp.concatenate([a for a, _ in split], axis=1)
    give = jnp.concatenate([b for _, b in split], axis=1)
    return side(ctx["core"], keep, swap(give, "core"))


def along_y(own):
    return swap(own, "ylo"), cross(own), swap(own, "section")


def both_layers(own, moved, ctx):
    near, crossed, facing = moved
    section, at_0 = ctx["section"], ctx["ylo"] == 0
    mine = (pick(at_0, own, near), pick(at_0, near, own))
    theirs = (pick(at_0, facing, crossed), pick(at_0, crossed, facing))
    first = [pick(section == 0, a, b) for a, b in zip(mine, theirs)]
    second = [pick(section == 0, b, a) for a, b in zip(mine, theirs)]
    return first, second


def y_then_x(own, moved, ctx, ready=()):
    first, second = both_layers(own, moved, ctx)
    return hold_by_corner(jnp.concatenate(first), *ready), jnp.concatenate(second)


def settle(grad):
    return lax.psum_scatter(row_major(grad), "x", scatter_dimension=0, tiled=True)


def sum_along_y(first, second, ctx):
    section, at_0 = ctx["section"], ctx["ylo"] == 0
    half = first.shape[0] // 2
    mine, theirs = pick(section == 0, first, second), pick(section == 0, second, first)
    keep, near = pick(at_0, mine[:half], mine[half:]), pick(at_0, mine[half:], mine[:half])
    facing, crossed = pick(at_0, theirs[:half], theirs[half:]), pick(at_0, theirs[half:], theirs[:half])
    return wide(keep) + wide(swap(near, "ylo")) + wide(swap(facing, "section")) + wide(cross(crossed))


def sum_across(first, second, ctx):
    section = ctx["section"]
    return wide(pick(section == 0, first, second)) + wide(cross(pick(section == 0, second, first)))


def share_out(total, ctx):
    core = ctx["core"]
    half = total.shape[0] // 2
    keep = pick(core == 0, total[:half], total[half:])
    give = pick(core == 0, total[half:], total[:half])
    return keep, wide(swap(low(give), "core"))


def both(pair, lo, hi, ctx):
    keep, other = pair
    a, b = keep[:, lo:hi], other[:, lo:hi]
    return jnp.where(ctx["core"] == 0, jnp.concatenate([a, b], 1), jnp.concatenate([b, a], 1))


def body(
    ends_in,
    segments,
    decay_rate,
    attn_gain,
    w_query,
    w_key,
    w_value,
    w_gate_ret,
    w_out,
    ffn_gain,
    w_gate,
    w_up,
    w_down,
):
    section, core, tensor = (lax.axis_index(a) for a in ("section", "core", "tensor"))
    x_at, ylo = lax.axis_index("x"), lax.axis_index("ylo")
    K, V, F = w_query.shape[2] // 2, w_value.shape[2] // 2, w_gate.shape[2] // 2
    D = w_query.shape[1] * lax.axis_size("x") * 4

    ends = ends_in[0]
    mine = pick(section == 0, ends[0], ends[1])
    theirs = swap(pick(section == 0, ends[1], ends[0]), "section")
    h0 = pick(section == 0, mine, theirs)
    g1 = pick(section == 0, theirs, mine)

    stretch = segments.shape[1]
    rows = 2 * stretch
    share = stretch // lax.axis_size("tensor")
    own_docs = pick(section == 0, segments[0], segments[1])
    ring = (tensor * share + jnp.arange(stretch)) % stretch
    own_docs = lax.dynamic_slice_in_dim(jnp.concatenate([own_docs, own_docs]), tensor * share, stretch)
    docs = jnp.concatenate([own_docs, swap(own_docs, "core")])
    places = jnp.concatenate([core * stretch + ring, (1 - core) * stretch + ring])
    block = x_at * 2 + ylo
    scale = K ** (-0.5)

    decays_all = decay_rate[0]
    decays_far = swap(decays_all, "section")
    head = tensor * 2 + core

    def context(layer, docs, rates_ready=()):
        rates = hold_by_corner(pick(section == layer, decays_all, decays_far)[None], *rates_ready)[0]
        rate = lax.dynamic_index_in_dim(rates, head, 0, False)
        gap = places[:, None] - places[None, :]
        allowed = (gap >= 0) & (docs[:, None] == docs[None, :])
        decay_mask = jnp.where(allowed, jnp.exp(-rate * jnp.where(allowed, gap, 0).astype(f32)), 0.0) * scale
        to_end = jnp.exp(-rate * (rows - 1 - places).astype(f32)) * (docs == jnp.max(docs))
        linked = (docs == jnp.min(docs)) & (block > 0)
        from_start = jnp.exp(-rate * (places + 1).astype(f32)) * linked * scale
        return {
            "decay_mask": decay_mask,
            "to_end": to_end[:, None],
            "from_start": from_start[:, None],
            "fade": jnp.exp(-rate * rows),
            "place": jnp.where(section == layer, ylo, 1 - ylo),
            "ylo": ylo,
            "core": core,
            "section": section,
            "sizes": (K, V, F),
        }

    ctx = {"ylo": ylo, "core": core, "section": section}

    gain_columns = jnp.stack([attn_gain[0], ffn_gain[0]], axis=1)
    gain_columns = jnp.concatenate([gain_columns, gain_columns], axis=1)
    with jax.named_scope("weights_key_value"):
        own_kv = pack((w_key[0], w_value[0], gain_columns), ctx)
        kv0, kv1 = y_then_x(own_kv, along_y(own_kv), ctx)
        kv0 = jnp.concatenate([kv0, kv1[:, K + V :]], axis=1)
    with jax.named_scope("weights_query_gate_out"):
        own_qgo = hold_by_corner(pack((w_query[0], w_gate_ret[0], w_out[0].T), ctx), kv0)
        moved_qgo = along_y(own_qgo)
    h0_rows = wide(spread(hold_by_corner(h0, moved_qgo[0])))
    ctx0 = context(0, docs)
    with jax.named_scope("weights_query_gate_out"):
        qgo0, qgo1 = y_then_x(own_qgo, moved_qgo, ctx, (h0_rows, ctx0["decay_mask"]))
    with jax.named_scope("gather_weights"):
        kv0, qgo0 = gather_x(kv0), gather_x(qgo0)
        in1 = gather_x(jnp.concatenate([kv1[:, : K + V], qgo1], axis=1))
    second = []

    def get_gud(pair):
        with jax.named_scope("weights_gate_up_down"):
            own_gud = columns_major(pack((w_gate[0], w_up[0], w_down[0].T), ctx))
            moved_gud = [columns_major(v) for v in along_y(own_gud)]
            gud0, gud1 = y_then_x(own_gud, moved_gud, ctx, (pair,))
            second.append(gather_x(gud1))
            return gather_x(gud0)

    gain_rows = wide(kv0[:, K + V :]).T
    gains0, gains1 = gain_rows[:2], gain_rows[2:]
    n_in = 2 * (K + V)
    weights0 = ((kv0, qgo0[:, : K + V]), qgo0[:, K + V :], get_gud)
    weights1 = ((in1[:, :n_in],), in1[:, n_in:], lambda pair: second[0])

    a0 = low(h0_rows * rms_inverse(h0_rows) * gains0[0])
    h0 = wide(h0)
    with jax.named_scope("layer0_forward"):
        record0, weights0 = forward(h0, a0, gains0[1], weights0, ctx0)
        out_first = layer_out(record0, weights0)
    h1 = wide(low(out_first))
    a1 = spread(low(h1 * rms_inverse(h1) * gains1[0]))
    ctx1 = context(1, docs, (h1,))
    def early_pairs(record, ctx):
        gated, hidden = record[2], record[3]
        got = swap(jnp.concatenate([gated, hidden], axis=1), "ylo")
        return (
            swap_half(record[0], ctx),
            swap_half(record[1], ctx),
            (gated, got[:, :V]),
            (hidden, got[:, V:]),
            got,
        )

    a_pair0, b_pair0, gated_pair0, hidden_pair0, got0 = early_pairs(record0, ctx0)
    d_f1 = spread(hold(g1, h1))
    f_pair1 = swap_half(d_f1, ctx1)
    a1 = hold(a1, a_pair0[1], b_pair0[1], got0, f_pair1[1])
    a_pair1 = swap_half(a1, ctx1)
    with jax.named_scope("layer1_forward"):
        waits = (a_pair1[1:], ())
        record1, weights1 = forward(h1, a1, gains1[1], weights1, ctx1, waits)
    a_pair1, b_pair1, gated_pair1, hidden_pair1, got1 = early_pairs(record1, ctx1)

    with jax.named_scope("layer1_out"):
        out_second = layer_out(record1, weights1)
    with jax.named_scope("layer1_backward"):
        waits = (
            lambda parts: (),
            lambda parts: b_pair1[1:],
            lambda parts: (out_second,),
            lambda parts: (got1, parts["gu"]),
        )
        pairs = a_pair1, b_pair1, f_pair1, gated_pair1, hidden_pair1
        d_h1, parts1, gain_grads1 = backward(
            h1, wide(g1), d_f1, record1, pairs, gains1, weights1, ctx1, waits
        )
    d_f0_rows = low(d_h1)
    def last_in(parts):
        return parts["in_partner"], parts["grad_in"]

    with jax.named_scope("layer0_backward"):
        d_f0 = spread(d_f0_rows)
        f_pair0 = swap_half(d_f0, ctx0)
        waits = (
            lambda parts: (parts1["in_partner"],),
            lambda parts: (f_pair0[1], parts1["od"]),
            lambda parts: (parts1["in"],),
            last_in,
        )
        pairs = a_pair0, b_pair0, f_pair0, gated_pair0, hidden_pair0
        d_h0, parts0, gain_grads0 = backward(
            h0, wide(d_f0_rows), d_f0, record0, pairs, gains0, weights0, ctx0, waits
        )
    gain_grads = jnp.stack(gain_grads0 + gain_grads1)

    def reduce_gains(*moves):
        with jax.named_scope("gains"):
            return gain_grads + sum(move(gain_grads) for move in moves)

    with jax.named_scope("owners"):
        gu = sum_across(parts0["gu"], parts1["gu"], ctx)
        gain_grads = hold(reduce_gains(*(lambda v, k=k: turn(v, "tensor", k) for k in (1, 2, 3))), gu)
        gain_grads = reduce_gains(lambda v: swap(v, "core"))
        gain_grads = reduce_gains(*(lambda v, k=k: turn(v, "x", k) for k in (1, 2, 3)))
        gain_grads = reduce_gains(lambda v: swap(v, "ylo"), cross, lambda v: swap(v, "section"))
        odqg1 = jnp.concatenate([parts1["od"], parts1["in"][:, K + V :]], axis=1)
        odqg = sum_across(parts0["od"], odqg1, ctx)
        kv = sum_across(parts0["in"], parts1["in"][:, : K + V], ctx)
        kv, odqg, gu = (share_out(total, ctx) for total in (kv, odqg, gu))
    grad_key = both(kv, 0, K, ctx)
    grad_value = both(kv, K, K + V, ctx)
    grad_out = both(odqg, 0, V, ctx).T
    grad_down = both(odqg, V, V + F, ctx).T
    grad_query = both(odqg, V + F, V + F + K, ctx)
    grad_gate_ret = both(odqg, V + F + K, V + F + K + V, ctx)
    grad_gate = both(gu, 0, F, ctx)
    grad_up = both(gu, F, 2 * F, ctx)

    own_gains = pick(section == 0, gain_grads[:2], gain_grads[2:])
    width = attn_gain.shape[1]
    own_gains = lax.dynamic_slice_in_dim(own_gains, (block * 2 + core) * width, width, 1)

    kept = pick(section == 0, d_h0, out_second)
    passed = swap(pick(section == 0, out_second, d_h0), "section")
    ends_out = jnp.where(section == 0, jnp.stack([kept, passed]), jnp.stack([passed, kept]))
    return (
        ends_out[None],
        own_gains[:1],
        grad_query[None],
        grad_key[None],
        grad_value[None],
        grad_gate_ret[None],
        grad_out[None],
        own_gains[1:],
        grad_gate[None],
        grad_up[None],
        grad_down[None],
    )


def solution(mesh):
    fine = Mesh(mesh.devices.reshape(2, 4, 2, 2, 4), AXES)
    by_rows = P("section", DP, "tensor")
    by_columns = P("section", "tensor", DP)
    ends = P("section", None, DP + ("tensor",), None)
    gain = P("section", DP)
    return jax.shard_map(
        body,
        mesh=fine,
        in_specs=(
            ends,
            P(None, DP),
            P("section", None),
            gain,
            by_rows,
            by_rows,
            by_rows,
            by_rows,
            by_columns,
            gain,
            by_rows,
            by_rows,
            by_columns,
        ),
        out_specs=(
            ends,
            gain,
            by_rows,
            by_rows,
            by_rows,
            by_rows,
            by_columns,
            gain,
            by_rows,
            by_rows,
            by_columns,
        ),
        check_vma=False,
    )
```

```python
import jax
import jax.numpy as jnp
from jax import lax
from jax.experimental import pallas as pl
from jax.experimental.layout import Layout, with_layout_constraint
from jax.sharding import Mesh, PartitionSpec as P

epsilon = 1e-06
group_floor = 1.0
AXES = ("section", "x", "ylo", "core", "tensor")
DP = ("x", "ylo", "core")
f32 = jnp.float32
bf16 = jnp.bfloat16


def low(v):
    return v.astype(bf16)


def wide(v):
    return v.astype(f32)


def row_major(v):
    return with_layout_constraint(v, Layout(major_to_minor=tuple(range(v.ndim))))


def columns_major(v):
    return with_layout_constraint(v, Layout(major_to_minor=(1, 0)))


def mm(a, b):
    return lax.dot_general(a, b, (((1,), (0,)), ((), ())), preferred_element_type=f32)


def mm_right(a, b):
    return lax.dot_general(a, b, (((1,), (1,)), ((), ())), preferred_element_type=f32)


def mm_left(a, b):
    return lax.dot_general(a, b, (((0,), (0,)), ((), ())), preferred_element_type=f32)


def swap(v, axis):
    return lax.ppermute(v, axis, [(0, 1), (1, 0)])


def cross(v):
    return lax.ppermute(v, ("section", "ylo"), [(0, 3), (1, 2), (2, 1), (3, 0)])


def turn(v, axis, by):
    n = lax.axis_size(axis)
    return lax.ppermute(v, axis, [(i, (i + by) % n) for i in range(n)])


def shift(v, axis, by):
    n = lax.axis_size(axis)
    return lax.ppermute(v, axis, [(i, i + by) for i in range(n) if 0 <= i + by < n])


def spread(rows):
    with jax.named_scope("spread"):
        return spread_rows(rows)


def collect(partial):
    with jax.named_scope("collect"):
        return collect_rows(partial)


def spread_rows(rows):
    n = lax.axis_size("tensor")
    rows = row_major(rows)
    parts = [rows] + [row_major(turn(rows, "tensor", -k)) for k in range(1, n)]
    own = row_major(jnp.concatenate(parts))
    return row_major(jnp.concatenate([own, row_major(swap(own, "core"))]))


def collect_rows(partial):
    n = lax.axis_size("tensor")
    half = partial.shape[0] // 2
    share = half // n
    partial = row_major(partial)
    own = row_major(partial[:half] + wide(swap(row_major(low(partial[half:])), "core")))
    total = own[:share]
    for k in range(1, n):
        total = total + wide(turn(row_major(low(own[k * share : (k + 1) * share])), "tensor", k))
    return row_major(total)


def pick(flag, a, b):
    return jnp.where(flag, a, b)


def side(flag, a, b):
    return jnp.where(flag == 0, jnp.concatenate([a, b]), jnp.concatenate([b, a]))


def rms_inverse(x):
    return lax.rsqrt(jnp.mean(x * x, axis=-1, keepdims=True) + epsilon)


def norm_back(x, gain, d_y):
    r = rms_inverse(x)
    gd = gain * d_y
    d_x = r * gd - x * (r * r * r) * jnp.mean(x * gd, axis=-1, keepdims=True)
    return d_x, jnp.sum(x * r * d_y, axis=0)


def earlier_states(state, ctx):
    with jax.named_scope("earlier_states"):
        return states_before(state, ctx)


def later_states(state, ctx):
    with jax.named_scope("later_states"):
        return states_after(state, ctx)


def states_before(state, ctx):
    fade = ctx["fade"]
    sent = low(state)
    got = swap(sent, "ylo")
    other = wide(got)
    own = wide(sent)
    y = ctx["ylo"]
    first, second = pick(y == 0, own, other), pick(y == 0, other, own)
    pair = low(fade * first + second)
    total = wide(shift(pair, "x", 1))
    total = total + (fade**2) * wide(shift(pair, "x", 2)) + (fade**4) * wide(shift(pair, "x", 3))
    return pick(y == 0, total, fade * total + first), pair


def states_after(state, ctx):
    fade = ctx["fade"]
    sent = low(state)
    other = wide(swap(sent, "ylo"))
    own = wide(sent)
    y = ctx["ylo"]
    first, second = pick(y == 0, own, other), pick(y == 0, other, own)
    pair = low(first + fade * second)
    total = wide(shift(pair, "x", -1))
    total = total + (fade**2) * wide(shift(pair, "x", -2)) + (fade**4) * wide(shift(pair, "x", -3))
    return pick(y == 1, total, second + fade * total)


def silu(v):
    return v * jax.nn.sigmoid(v)


def forward(h, a_rows, ffn_gain, weights, ctx, waits=((), ())):
    w_in, w_out, get_gud = weights
    K, V, F = ctx["sizes"]
    split = len(w_in) == 2
    kv = mm(a_rows, w_in[0])
    k, v = low(kv[:, :K]), low(kv[:, K : K + V])
    faded_k = low(wide(k) * ctx["to_end"])
    state_in, pair = earlier_states(mm_left(faded_k, v), ctx)
    state_in = low(state_in)
    w_gud = get_gud(pair)
    w_gu, w_down = w_gud[:, : 2 * F], w_gud[:, 2 * F :]
    qg = mm(a_rows, w_in[1]) if split else kv[:, K + V :]
    q, ret_gate = low(qg[:, :K]), qg[:, K:]
    scores = low(mm_right(q, k) * ctx["decay_mask"])
    retained = mm(scores, v) + mm(q, state_in) * ctx["from_start"]
    n = lax.rsqrt(jnp.mean(retained * retained, axis=-1, keepdims=True) + group_floor)
    gated = low(silu(ret_gate) * (retained * n))
    mid = hold(h + collect(mm_right(gated, w_out)), *waits[0])
    b_rows = hold(spread(low(mid * rms_inverse(mid) * ffn_gain)), *waits[1])
    gu = mm(b_rows, w_gu)
    gate_pre, up_pre = gu[:, :F], gu[:, F:]
    hidden = low(silu(gate_pre) * up_pre)
    record = (a_rows, b_rows, gated, hidden, k, v, q, state_in, scores, ret_gate, retained, mid, gu)
    return record, (w_in, w_out, w_gu, w_down)


def layer_out(record, weights):
    hidden, mid = record[3], record[-2]
    return mid + collect(mm_right(hidden, weights[-1]))


def backward(h, g_out, d_f, record, pairs, gains, weights, ctx, waits):
    a_pair, b_pair, f_pair, gated_pair, hidden_pair = pairs
    w_in, w_out, w_gu, w_down = weights
    attn_gain, ffn_gain = gains
    K, V, F = ctx["sizes"]
    a_rows, b_rows, gated, hidden, k, v, q, state_in, scores, ret_gate, retained, mid, gu = record
    split = len(w_in) == 2
    parts = {}
    d_hidden = mm(d_f, w_down)
    gate_pre, up_pre = gu[:, :F], gu[:, F:]
    s = jax.nn.sigmoid(gate_pre)
    d_gate = low(d_hidden * up_pre * s * (1.0 + gate_pre * (1.0 - s)))
    d_up = low(d_hidden * gate_pre * s)
    d_gu = jnp.concatenate([d_gate, d_up], axis=1)
    gu_pair = with_partner(d_gu)
    d_b = hold(collect(mm_right(d_gu, w_gu)), gu_pair[1], *waits[0](parts))
    parts["gu"] = settle(weight_grad(b_pair, gu_pair))
    d_norm, grad_ffn_gain = norm_back(mid, ffn_gain, d_b)
    d_mid = g_out + d_norm
    d_r = hold(spread(low(d_mid)), *waits[1](parts))
    r_pair = swap_half(d_r, ctx)
    d_gated = mm(d_r, w_out)
    s = jax.nn.sigmoid(ret_gate)
    n = lax.rsqrt(jnp.mean(retained * retained, axis=-1, keepdims=True) + group_floor)
    d_ret_gate = low(d_gated * (retained * n) * s * (1.0 + ret_gate * (1.0 - s)))
    d_normed = d_gated * ret_gate * s
    d_ret = n * d_normed - retained * (n * n * n) * jnp.mean(
        retained * d_normed, axis=-1, keepdims=True
    )
    d_ret_low = low(d_ret)
    d_ret_start = low(d_ret * ctx["from_start"])
    beyond = low(later_states(mm_left(q, d_ret_start), ctx))
    d_scores = low(mm_right(d_ret_low, v) * ctx["decay_mask"])
    d_q = low(mm(d_scores, k) + mm_right(d_ret_start, state_in))
    d_qg = jnp.concatenate([d_q, d_ret_gate], axis=1)
    grads = [weight_grad(r_pair, gated_pair), weight_grad(f_pair, hidden_pair)]
    swapped = [r_pair[1]]
    if split:
        qg_pair = with_partner(d_qg)
        swapped.append(qg_pair[1])
        grads.append(weight_grad(a_pair, qg_pair))
    grad_od = row_major(jnp.concatenate(grads, axis=1))
    parts["od"] = settle(grad_od)
    beyond = hold(beyond, *swapped, *waits[2](parts))
    d_k = low(mm_left(d_scores, q) + mm_right(v, beyond) * ctx["to_end"])
    d_v = low(mm_left(scores, d_ret_low) + mm(k, beyond) * ctx["to_end"])
    d_kv = jnp.concatenate([d_k, d_v], axis=1)
    d_in = d_kv if split else jnp.concatenate([d_kv, d_qg], axis=1)
    if split:
        d_kv_wide = jnp.pad(d_kv, ((0, 0), (0, w_in[0].shape[1] - d_kv.shape[1])))
        partial = mm_right(d_qg, w_in[1]) + mm_right(d_kv_wide, w_in[0])
    else:
        partial = mm_right(d_in, w_in[0])
    in_pair = with_partner(d_in)
    parts["in_partner"] = in_pair[1]
    if split:
        in_pair = in_pair[0], hold(in_pair[1], grad_od)
    parts["grad_in"] = weight_grad(a_pair, in_pair)
    parts["in"] = settle(parts["grad_in"])
    d_a = hold(collect(partial), *waits[3](parts))
    d_norm, grad_attn_gain = norm_back(h, attn_gain, d_a)
    return d_mid + d_norm, parts, (grad_attn_gain, grad_ffn_gain)


def with_partner(v):
    return v, swap(v, "ylo")


def swap_half(v, ctx):
    n = lax.axis_size("x")
    width = v.shape[1] // (2 * n)
    cut = [v[:, i * width : (i + 1) * width] for i in range(2 * n)]

    def half(which):
        return jnp.concatenate([pick(which == 0, cut[2 * i], cut[2 * i + 1]) for i in range(n)], axis=1)

    place = ctx["place"]
    return half(place), swap(half(1 - place), "ylo")


def weight_grad(left, right):
    return row_major(low(mm_left(left[0], right[0]) + mm_left(left[1], right[1])))


def halves(w, core):
    n = w.shape[1] // 2
    first, second = w[:, :n], w[:, n:]
    return pick(core == 0, first, second), pick(core == 0, second, first)


def hold(v, *others):
    if not others:
        return v
    anywhere = pl.BlockSpec(memory_space=pl.ANY)
    return pl.pallas_call(
        lambda *refs: None,
        out_shape=jax.ShapeDtypeStruct(v.shape, v.dtype),
        in_specs=[anywhere] * (1 + len(others)),
        out_specs=anywhere,
        input_output_aliases={0: 0},
        cost_estimate=pl.CostEstimate(flops=0, bytes_accessed=0, transcendentals=0),
    )(v, *others)


def corner(v):
    return v[tuple(slice(n - 1, n) for n in v.shape)].reshape(1, 1)


def hold_by_corner(v, *others):
    if not others:
        return v
    corners = [corner(other) for other in others]
    bad = corners[0] != corners[0]
    for c in corners[1:]:
        bad = bad | (c != c)
    return jnp.where(bad, jnp.zeros((), v.dtype), v)


def gather_x(rows):
    return lax.all_gather(rows, "x", axis=0, tiled=True)


def pack(shards, ctx):
    split = [halves(w, ctx["core"]) for w in shards]
    keep = jnp.concatenate([a for a, _ in split], axis=1)
    give = jnp.concatenate([b for _, b in split], axis=1)
    return side(ctx["core"], keep, swap(give, "core"))


def along_y(own):
    return swap(own, "ylo"), cross(own), swap(own, "section")


def both_layers(own, moved, ctx):
    near, crossed, facing = moved
    section, at_0 = ctx["section"], ctx["ylo"] == 0
    mine = (pick(at_0, own, near), pick(at_0, near, own))
    theirs = (pick(at_0, facing, crossed), pick(at_0, crossed, facing))
    first = [pick(section == 0, a, b) for a, b in zip(mine, theirs)]
    second = [pick(section == 0, b, a) for a, b in zip(mine, theirs)]
    return first, second


def y_then_x(own, moved, ctx, ready=()):
    first, second = both_layers(own, moved, ctx)
    return hold_by_corner(jnp.concatenate(first), *ready), jnp.concatenate(second)


def settle(grad):
    return lax.psum_scatter(row_major(grad), "x", scatter_dimension=0, tiled=True)


def sum_along_y(first, second, ctx):
    section, at_0 = ctx["section"], ctx["ylo"] == 0
    half = first.shape[0] // 2
    mine, theirs = pick(section == 0, first, second), pick(section == 0, second, first)
    keep, near = pick(at_0, mine[:half], mine[half:]), pick(at_0, mine[half:], mine[:half])
    facing, crossed = pick(at_0, theirs[:half], theirs[half:]), pick(at_0, theirs[half:], theirs[:half])
    return wide(keep) + wide(swap(near, "ylo")) + wide(swap(facing, "section")) + wide(cross(crossed))


def sum_across(first, second, ctx):
    section = ctx["section"]
    return wide(pick(section == 0, first, second)) + wide(cross(pick(section == 0, second, first)))


def share_out(total, ctx):
    core = ctx["core"]
    half = total.shape[0] // 2
    keep = pick(core == 0, total[:half], total[half:])
    give = pick(core == 0, total[half:], total[:half])
    return keep, wide(swap(low(give), "core"))


def both(pair, lo, hi, ctx):
    keep, other = pair
    a, b = keep[:, lo:hi], other[:, lo:hi]
    return jnp.where(ctx["core"] == 0, jnp.concatenate([a, b], 1), jnp.concatenate([b, a], 1))


def body(
    ends_in,
    segments,
    decay_rate,
    attn_gain,
    w_query,
    w_key,
    w_value,
    w_gate_ret,
    w_out,
    ffn_gain,
    w_gate,
    w_up,
    w_down,
):
    section, core, tensor = (lax.axis_index(a) for a in ("section", "core", "tensor"))
    x_at, ylo = lax.axis_index("x"), lax.axis_index("ylo")
    K, V, F = w_query.shape[2] // 2, w_value.shape[2] // 2, w_gate.shape[2] // 2
    D = w_query.shape[1] * lax.axis_size("x") * 4

    ends = ends_in[0]
    mine = pick(section == 0, ends[0], ends[1])
    theirs = swap(pick(section == 0, ends[1], ends[0]), "section")
    h0 = pick(section == 0, mine, theirs)
    g1 = pick(section == 0, theirs, mine)

    stretch = segments.shape[1]
    rows = 2 * stretch
    share = stretch // lax.axis_size("tensor")
    own_docs = pick(section == 0, segments[0], segments[1])
    ring = (tensor * share + jnp.arange(stretch)) % stretch
    own_docs = lax.dynamic_slice_in_dim(jnp.concatenate([own_docs, own_docs]), tensor * share, stretch)
    docs = jnp.concatenate([own_docs, swap(own_docs, "core")])
    places = jnp.concatenate([core * stretch + ring, (1 - core) * stretch + ring])
    block = x_at * 2 + ylo
    scale = K ** (-0.5)

    decays_all = decay_rate[0]
    decays_far = swap(decays_all, "section")
    head = tensor * 2 + core

    def context(layer, docs, rates_ready=()):
        rates = hold_by_corner(pick(section == layer, decays_all, decays_far)[None], *rates_ready)[0]
        rate = lax.dynamic_index_in_dim(rates, head, 0, False)
        gap = places[:, None] - places[None, :]
        allowed = (gap >= 0) & (docs[:, None] == docs[None, :])
        decay_mask = jnp.where(allowed, jnp.exp(-rate * jnp.where(allowed, gap, 0).astype(f32)), 0.0) * scale
        to_end = jnp.exp(-rate * (rows - 1 - places).astype(f32)) * (docs == jnp.max(docs))
        linked = (docs == jnp.min(docs)) & (block > 0)
        from_start = jnp.exp(-rate * (places + 1).astype(f32)) * linked * scale
        return {
            "decay_mask": decay_mask,
            "to_end": to_end[:, None],
            "from_start": from_start[:, None],
            "fade": jnp.exp(-rate * rows),
            "place": jnp.where(section == layer, ylo, 1 - ylo),
            "ylo": ylo,
            "core": core,
            "section": section,
            "sizes": (K, V, F),
        }

    ctx = {"ylo": ylo, "core": core, "section": section}

    gain_columns = jnp.stack([attn_gain[0], ffn_gain[0]], axis=1)
    gain_columns = jnp.concatenate([gain_columns, gain_columns], axis=1)
    with jax.named_scope("weights_key_value"):
        own_kv = pack((w_key[0], w_value[0], gain_columns), ctx)
        kv0, kv1 = y_then_x(own_kv, along_y(own_kv), ctx)
        kv0 = jnp.concatenate([kv0, kv1[:, K + V :]], axis=1)
    with jax.named_scope("weights_query_gate_out"):
        own_qgo = hold_by_corner(pack((w_query[0], w_gate_ret[0], w_out[0].T), ctx), kv0)
        moved_qgo = along_y(own_qgo)
    h0_rows = wide(spread(hold_by_corner(h0, moved_qgo[0])))
    ctx0 = context(0, docs)
    with jax.named_scope("weights_query_gate_out"):
        qgo0, qgo1 = y_then_x(own_qgo, moved_qgo, ctx, (h0_rows, ctx0["decay_mask"]))
    with jax.named_scope("gather_weights"):
        kv0, qgo0 = gather_x(kv0), gather_x(qgo0)
        in1 = gather_x(jnp.concatenate([kv1[:, : K + V], qgo1], axis=1))
    second = []

    def get_gud(pair):
        with jax.named_scope("weights_gate_up_down"):
            own_gud = columns_major(pack((w_gate[0], w_up[0], w_down[0].T), ctx))
            moved_gud = [columns_major(v) for v in along_y(own_gud)]
            gud0, gud1 = y_then_x(own_gud, moved_gud, ctx, (pair,))
            second.append(gather_x(gud1))
            return gather_x(gud0)

    gain_rows = wide(kv0[:, K + V :]).T
    gains0, gains1 = gain_rows[:2], gain_rows[2:]
    n_in = 2 * (K + V)
    weights0 = ((kv0, qgo0[:, : K + V]), qgo0[:, K + V :], get_gud)
    weights1 = ((in1[:, :n_in],), in1[:, n_in:], lambda pair: second[0])

    a0 = low(h0_rows * rms_inverse(h0_rows) * gains0[0])
    h0 = wide(h0)
    with jax.named_scope("layer0_forward"):
        record0, weights0 = forward(h0, a0, gains0[1], weights0, ctx0)
        out_first = layer_out(record0, weights0)
    h1 = wide(low(out_first))
    a1 = spread(low(h1 * rms_inverse(h1) * gains1[0]))
    ctx1 = context(1, docs, (h1,))
    def early_pairs(record, ctx):
        gated, hidden = record[2], record[3]
        got = swap(jnp.concatenate([gated, hidden], axis=1), "ylo")
        return (
            swap_half(record[0], ctx),
            swap_half(record[1], ctx),
            (gated, got[:, :V]),
            (hidden, got[:, V:]),
            got,
        )

    a_pair0, b_pair0, gated_pair0, hidden_pair0, got0 = early_pairs(record0, ctx0)
    d_f1 = spread(hold(g1, h1))
    f_pair1 = swap_half(d_f1, ctx1)
    a1 = hold(a1, a_pair0[1], b_pair0[1], f_pair1[1])
    a_pair1 = swap_half(a1, ctx1)
    with jax.named_scope("layer1_forward"):
        waits = (a_pair1[1:], (got0,))
        record1, weights1 = forward(h1, a1, gains1[1], weights1, ctx1, waits)
    a_pair1, b_pair1, gated_pair1, hidden_pair1, got1 = early_pairs(record1, ctx1)

    with jax.named_scope("layer1_out"):
        out_second = layer_out(record1, weights1)
    with jax.named_scope("layer1_backward"):
        waits = (
            lambda parts: (),
            lambda parts: b_pair1[1:],
            lambda parts: (out_second,),
            lambda parts: (got1, parts["gu"]),
        )
        pairs = a_pair1, b_pair1, f_pair1, gated_pair1, hidden_pair1
        d_h1, parts1, gain_grads1 = backward(
            h1, wide(g1), d_f1, record1, pairs, gains1, weights1, ctx1, waits
        )
    d_f0_rows = low(d_h1)
    def last_in(parts):
        return parts["in_partner"], parts["grad_in"]

    with jax.named_scope("layer0_backward"):
        d_f0 = spread(d_f0_rows)
        f_pair0 = swap_half(d_f0, ctx0)
        waits = (
            lambda parts: (parts1["in_partner"],),
            lambda parts: (f_pair0[1], parts1["od"]),
            lambda parts: (parts1["in"],),
            last_in,
        )
        pairs = a_pair0, b_pair0, f_pair0, gated_pair0, hidden_pair0
        d_h0, parts0, gain_grads0 = backward(
            h0, wide(d_f0_rows), d_f0, record0, pairs, gains0, weights0, ctx0, waits
        )
    gain_grads = jnp.stack(gain_grads0 + gain_grads1)

    def reduce_gains(*moves):
        with jax.named_scope("gains"):
            return gain_grads + sum(move(gain_grads) for move in moves)

    with jax.named_scope("owners"):
        gu = sum_across(parts0["gu"], parts1["gu"], ctx)
        gain_grads = hold(reduce_gains(*(lambda v, k=k: turn(v, "tensor", k) for k in (1, 2, 3))), gu)
        gain_grads = reduce_gains(lambda v: swap(v, "core"))
        gain_grads = reduce_gains(*(lambda v, k=k: turn(v, "x", k) for k in (1, 2, 3)))
        gain_grads = reduce_gains(lambda v: swap(v, "ylo"), cross, lambda v: swap(v, "section"))
        odqg1 = jnp.concatenate([parts1["od"], parts1["in"][:, K + V :]], axis=1)
        odqg = sum_across(parts0["od"], odqg1, ctx)
        kv = sum_across(parts0["in"], parts1["in"][:, : K + V], ctx)
        kv, odqg, gu = (share_out(total, ctx) for total in (kv, odqg, gu))
    grad_key = both(kv, 0, K, ctx)
    grad_value = both(kv, K, K + V, ctx)
    grad_out = both(odqg, 0, V, ctx).T
    grad_down = both(odqg, V, V + F, ctx).T
    grad_query = both(odqg, V + F, V + F + K, ctx)
    grad_gate_ret = both(odqg, V + F + K, V + F + K + V, ctx)
    grad_gate = both(gu, 0, F, ctx)
    grad_up = both(gu, F, 2 * F, ctx)

    own_gains = pick(section == 0, gain_grads[:2], gain_grads[2:])
    width = attn_gain.shape[1]
    own_gains = lax.dynamic_slice_in_dim(own_gains, (block * 2 + core) * width, width, 1)

    kept = pick(section == 0, d_h0, out_second)
    passed = swap(pick(section == 0, out_second, d_h0), "section")
    ends_out = jnp.where(section == 0, jnp.stack([kept, passed]), jnp.stack([passed, kept]))
    return (
        ends_out[None],
        own_gains[:1],
        grad_query[None],
        grad_key[None],
        grad_value[None],
        grad_gate_ret[None],
        grad_out[None],
        own_gains[1:],
        grad_gate[None],
        grad_up[None],
        grad_down[None],
    )


def solution(mesh):
    fine = Mesh(mesh.devices.reshape(2, 4, 2, 2, 4), AXES)
    by_rows = P("section", DP, "tensor")
    by_columns = P("section", "tensor", DP)
    ends = P("section", None, DP + ("tensor",), None)
    gain = P("section", DP)
    return jax.shard_map(
        body,
        mesh=fine,
        in_specs=(
            ends,
            P(None, DP),
            P("section", None),
            gain,
            by_rows,
            by_rows,
            by_rows,
            by_rows,
            by_columns,
            gain,
            by_rows,
            by_rows,
            by_columns,
        ),
        out_specs=(
            ends,
            gain,
            by_rows,
            by_rows,
            by_rows,
            by_rows,
            by_columns,
            gain,
            by_rows,
            by_rows,
            by_columns,
        ),
        check_vma=False,
    )
```
